1024 devices in a mesh: dp: 4 (over y), expert: 32 (over x, z_lo), mp: 8 (over z_hi, core).
Axes of the slice: x: 4, y: 4, z: 32 (z_hi: 4, z_lo: 8; z = z_hi * 8 + z_lo), core: 2. Of those that a mesh axis runs over, the one named last changes fastest.
Arguments:
- tokens: bfloat16 [16384, 2048], P(('dp', 'expert')), may hold values from -6 to 6
- cotangent: bfloat16 [16384, 2048], P(('dp', 'expert')), may hold values from -1.5 to 1.5
- gate_value: float32 [16384], P(('dp', 'expert')), may hold values from 0.25 to 1
- expert_id: int32 [16384], P(('dp', 'expert')), may hold values from 0 to 31, as said below
- token_slot: int32 [16384], P(('dp', 'expert')), may hold values from -1 to 3, as said below
- w_in: bfloat16 [32, 2048, 5120], P('expert', 'dp', 'mp'), may hold values from -0.125 to 0.125
- w_out: bfloat16 [32, 5120, 2048], P('expert', 'mp', 'dp'), may hold values from -0.078125 to 0.078125
Outputs:
- grad_tokens: bfloat16 [16384, 4, 512], P(('dp', 'expert'), None, 'mp')
- grad_w_in: bfloat16 [32, 2048, 5120], P('expert', 'dp', 'mp')
- grad_w_out: bfloat16 [32, 5120, 2048], P('expert', 'mp', 'dp')
The draws below stay inside these ranges and needn't reach their ends.
Inputs may be any that keep to these rules, and one draw needn't show every extreme that they name: `expert_id`: in every group of 128 consecutive tokens some expert is named by 4 + 1 tokens or more. `token_slot`: A kept token's slot counts the earlier tokens of its group that name the same expert; tokens whose count reaches 4 have slot -1. Every group drops tokens, and some expert has all 4 slots used by every group.
All inputs are finite; a program needn't handle non-finite values.
Results may differ from the reference program's by a relative error of at most 0.025.
Values may be sent and summed in bfloat16 or wider, within the bound.
No kernel may reach another device: no remote copies, remote signals or barrier semaphores. Data moves between devices by JAX's collectives and lax.ppermute only.
A program may use at most 32 MiB of HBM per device.

```python
import jax
import jax.numpy as jnp
from jax import lax

D = 2048
FF = 5120
TOK_DEV = 128
EXPERTS = 32
REPLICAS = 4
SLICES = 8
CAP = 4
ROWS = 512
TOKENS = 16384
N_EXPERT = 32


def route_table(key):
    groups = TOKENS // TOK_DEV
    key_one, key_two, key_three, key_four = jax.random.split(key, 4)
    low_pick = jnp.minimum(jax.random.randint(key_one, (groups, TOK_DEV), 0, EXPERTS), jax.random.randint(key_two, (groups, TOK_DEV), 0, EXPERTS))
    relabel = jax.random.permutation(key_three, EXPERTS)
    chosen = relabel[low_pick]
    forced = jax.random.randint(key_four, (), 0, EXPERTS)
    position = jnp.arange(TOK_DEV, dtype=jnp.int32)[None, :]
    chosen = jnp.where(position <= CAP, forced, chosen).astype(jnp.int32)
    onehot = (chosen[:, :, None] == jnp.arange(EXPERTS, dtype=jnp.int32)[None, None, :]).astype(jnp.int32)
    rank_run = jnp.cumsum(onehot, axis=1) - 1
    own_rank = jnp.sum(rank_run * onehot, axis=2)
    slot_ids = jnp.where(own_rank < CAP, own_rank, -1).astype(jnp.int32)
    return (chosen.reshape(TOKENS), slot_ids.reshape(TOKENS))


def draw_expert_id(key, part):
    chosen, slot_ids = route_table(key)
    return chosen


def draw_token_slot(key, part):
    chosen, slot_ids = route_table(key)
    return slot_ids


def block_levels(rng, shape, shards, least, largest):
    def one(axis_at, parts):
        heights = jax.random.uniform(jax.random.fold_in(jax.random.fold_in(rng, 6), axis_at), (parts,), jnp.float32, least / len(shards), largest / len(shards))
        return jnp.repeat(jnp.exp(heights), shape[axis_at] // parts).reshape((-1,) + (1,) * (len(shape) - axis_at - 1))

    level = one(*shards[0])
    for cut in shards[1:]:
        level = level * one(*cut)
    return level


def normal_values(key, extent, deviation, reach, pieces=(), held_as=jnp.bfloat16):
    result = jax.random.normal(key, extent, jnp.float32) * deviation
    if len(pieces) > 0:
        result = block_levels(key, extent, pieces, -0.22, 0.18) * result
    return jnp.clip(result, min=-reach, max=reach).astype(held_as)


def setup_inputs(seed: int = 0) -> dict:
    seeds = jax.random.split(jax.random.key(seed), 8)
    return {
        "tokens": normal_values(seeds[0], (TOKENS, D), 1.0, 6.0, ((0, 128),)),
        "cotangent": normal_values(seeds[1], (TOKENS, D), 0.25, 1.5, ((0, 128),)),
        "gate_value": jnp.clip(0.25 + 0.75 * jax.random.uniform(seeds[2], (TOKENS,), jnp.float32) ** block_levels(seeds[2], (TOKENS,), ((0, 128),), -0.2, 0.2), 0.25, 1.0),
        "expert_id": draw_expert_id(jax.random.fold_in(seeds[7], 71), 0),
        "token_slot": draw_token_slot(jax.random.fold_in(seeds[7], 71), 0),
        "w_in": normal_values(seeds[5], (EXPERTS, D, FF), D ** -0.5, 0.125, ((0, 32), (1, 4), (2, 8))),
        "w_out": normal_values(seeds[6], (EXPERTS, FF, D), FF ** -0.5, 0.078125, ((0, 32), (1, 8), (2, 4))),
    }


tanh_scale = 0.7978845608028654
cubic_coef = 0.044715


def gelu_pair(pre_act):
    tanh_arg = tanh_scale * (pre_act + cubic_coef * pre_act * pre_act * pre_act)
    tanh_val = jnp.tanh(tanh_arg)
    gelu_value = 0.5 * pre_act * (1.0 + tanh_val)
    gelu_slope = 0.5 * (1.0 + tanh_val) + 0.5 * pre_act * (1.0 - tanh_val * tanh_val) * tanh_scale * (1.0 + 3.0 * cubic_coef * pre_act * pre_act)
    return gelu_value, gelu_slope


def one_expert(operands):
    expert_x, expert_dy, weight_in, weight_out = operands
    quarter = D // REPLICAS
    x_blocks = expert_x.astype(jnp.float32).reshape(ROWS, REPLICAS, quarter)
    dy_blocks = expert_dy.astype(jnp.float32).reshape(ROWS, REPLICAS, quarter)
    win_blocks = weight_in.astype(jnp.float32).reshape(REPLICAS, quarter, FF)
    wout_blocks = weight_out.astype(jnp.float32).reshape(FF, REPLICAS, quarter)
    hidden_part = jnp.einsum("rqd,qdf->qrf", x_blocks, win_blocks).astype(jnp.bfloat16)
    pre_act = jnp.sum(hidden_part.astype(jnp.float32), axis=0)
    back_part = jnp.einsum("rqd,fqd->qrf", dy_blocks, wout_blocks).astype(jnp.bfloat16)
    grad_act = jnp.sum(back_part.astype(jnp.float32), axis=0)
    gelu_value, gelu_slope = gelu_pair(pre_act)
    activation = gelu_value.astype(jnp.bfloat16)
    d_hidden = (grad_act * gelu_slope).astype(jnp.bfloat16)
    grad_in = jnp.dot(expert_x.T, d_hidden, preferred_element_type=jnp.float32).astype(jnp.bfloat16)
    grad_out = jnp.dot(activation.T, expert_dy, preferred_element_type=jnp.float32).astype(jnp.bfloat16)
    slice_width = FF // SLICES
    dh_blocks = d_hidden.astype(jnp.float32).reshape(ROWS, SLICES, slice_width)
    w_slices = weight_in.astype(jnp.float32).reshape(D, SLICES, slice_width)
    row_part = jnp.einsum("rmf,dmf->mrd", dh_blocks, w_slices).astype(jnp.bfloat16)
    d_rows = jnp.sum(row_part.astype(jnp.float32), axis=0).astype(jnp.bfloat16)
    return grad_in, grad_out, d_rows


def reference(tokens, cotangent, gate_value, expert_id, token_slot, w_in, w_out):
    group_id = jnp.arange(TOKENS, dtype=jnp.int32) // TOK_DEV
    replica = group_id // N_EXPERT
    source = group_id % N_EXPERT
    is_kept = token_slot >= 0
    target = jnp.where(is_kept, expert_id * ROWS + (source * REPLICAS + replica) * CAP + token_slot, EXPERTS * ROWS).astype(jnp.int32)
    gated_dy = (gate_value[:, None] * cotangent.astype(jnp.float32)).astype(jnp.bfloat16)
    zero_rows = jnp.zeros((EXPERTS * ROWS + 1, D), jnp.bfloat16)
    disp_x = zero_rows.at[target].set(tokens)[:-1].reshape(EXPERTS, ROWS, D)
    disp_dy = zero_rows.at[target].set(gated_dy)[:-1].reshape(EXPERTS, ROWS, D)
    grad_w_in, grad_w_out, d_rows = lax.map(one_expert, (disp_x, disp_dy, w_in, w_out))
    flat_rows = jnp.concatenate([d_rows.reshape(EXPERTS * ROWS, D), jnp.zeros((1, D), jnp.bfloat16)], axis=0)
    grad_tokens = flat_rows[target].reshape(TOKENS, REPLICAS, D // REPLICAS)
    return grad_tokens, grad_w_in, grad_w_out
```

```python
import jax
import jax.numpy as jnp
from jax import lax
from jax.experimental import pallas as pl
from jax.experimental.pallas import tpu as pltpu
from jax.sharding import Mesh, PartitionSpec as P

tanh_scale = 0.7978845608028654
cubic_coef = 0.044715
f32 = jnp.float32
bf16 = jnp.bfloat16


def gelu_pair(pre_act):
    tanh_arg = tanh_scale * (pre_act + cubic_coef * pre_act * pre_act * pre_act)
    tanh_val = jnp.tanh(tanh_arg)
    gelu_value = 0.5 * pre_act * (1.0 + tanh_val)
    gelu_slope = 0.5 * (1.0 + tanh_val) + 0.5 * pre_act * (
        1.0 - tanh_val * tanh_val
    ) * tanh_scale * (1.0 + 3.0 * cubic_coef * pre_act * pre_act)
    return (gelu_value, gelu_slope)


def dot(a, b, dims):
    return lax.dot_general(a, b, ((dims[0], dims[1]), ((), ())), preferred_element_type=f32)


def call(kernel, outs, *args, flops=0):
    moved = sum(a.size * a.dtype.itemsize for a in args) + sum(
        jnp.dtype(d).itemsize * size(s) for s, d in outs
    )
    core = lax.axis_index("c").astype(jnp.int32).reshape(1)
    return pl.pallas_call(
        kernel,
        out_shape=[jax.ShapeDtypeStruct(s, d) for s, d in outs],
        in_specs=[pl.BlockSpec(memory_space=pltpu.SMEM)]
        + [pl.BlockSpec(memory_space=pltpu.VMEM)] * len(args),
        out_specs=[pl.BlockSpec(memory_space=pltpu.VMEM)] * len(outs),
        compiler_params=pltpu.CompilerParams(vmem_limit_bytes=32 * 1024 * 1024),
        cost_estimate=pl.CostEstimate(flops=flops, bytes_accessed=moved, transcendentals=0),
    )(core, *args)


def size(shape):
    n = 1
    for s in shape:
        n *= s
    return n


def slot_onehot(expert_id, token_slot, half, rows):
    low = token_slot - 2 * half
    target = jnp.where((low >= 0) & (low < 2), expert_id * 2 + low, -1)
    at = lax.broadcasted_iota(jnp.int32, (rows, expert_id.shape[1]), 0)
    return at == target


def dispatch_kernel(core, eid, slot, gate, tok, cot, out):
    quarters, feats = 4, out.shape[3]
    xs, rows = out.shape[0] // quarters, out.shape[2]
    hit = slot_onehot(eid[...], slot[...], core[0], xs * rows)
    onehot = hit.astype(f32).astype(bf16)
    row_gate = jnp.sum(jnp.where(hit, gate[...], 0.0), axis=1, keepdims=True)
    for q in range(quarters):
        cols = slice(q * feats, (q + 1) * feats)
        got_x = dot(onehot, tok[:, cols], ((1,), (0,))).astype(bf16)
        got_dy = (row_gate * dot(onehot, cot[:, cols], ((1,), (0,)))).astype(bf16)
        for x in range(xs):
            out[q * xs + x, 0] = got_x[x * rows : (x + 1) * rows]
            out[q * xs + x, 1] = got_dy[x * rows : (x + 1) * rows]


def swap_matrix(outer, inner):
    n = outer * inner * 2
    row = lax.broadcasted_iota(jnp.int32, (n, n), 0)
    col = lax.broadcasted_iota(jnp.int32, (n, n), 1)
    pair = row // 2
    source = ((pair % outer) * inner + pair // outer) * 2 + row % 2
    return (source == col).astype(f32).astype(bf16)


def regroup_kernel(core, got, out):
    perm = swap_matrix(got.shape[0], out.shape[0])
    n = perm.shape[0]
    for which in range(2):
        rows = got[:, which].reshape(n, -1)
        moved = dot(perm, rows, ((1,), (0,))).astype(bf16)
        out[:, which] = moved.reshape(out.shape[0], out.shape[2], -1)


def parts_kernel(core, own, other, w_in, w_out, out):
    half = out.shape[0] // 2
    hid = w_in.shape[1]
    for at, src in ((0, own), (half, other)):
        x = src[:, 0].reshape(half, -1)
        dy = src[:, 1].reshape(half, -1)
        out[at : at + half, :hid] = dot(x, w_in[...], ((1,), (0,))).astype(bf16)
        out[at : at + half, hid:] = dot(dy, w_out[...], ((1,), (1,))).astype(bf16)


def gelu_kernel(core, got, dh, act):
    hid = dh.shape[2]
    total = got[0].astype(f32)
    for q in range(1, got.shape[0]):
        total = total + got[q].astype(f32)
    gelu_value, gelu_slope = gelu_pair(total[:, :hid])
    activation = gelu_value.astype(bf16)
    d_hidden = (total[:, hid:] * gelu_slope).astype(bf16)
    for q in range(got.shape[0]):
        dh[q] = d_hidden
        act[q] = activation


def back_kernel(core, dh, w_in, mine, theirs):
    hs, block = 4, w_in.shape[0] // 8
    for out, c in ((theirs, 1 - core[0]), (mine, core[0])):
        w = jnp.concatenate(
            [
                w_in[pl.ds(pl.multiple_of(h * 2 * block + c * block, block), block), :]
                for h in range(hs)
            ],
            axis=0,
        )
        out[...] = dot(dh[...], w, ((1,), (1,))).astype(out.dtype)


def pack_kernel(core, mine, got, out):
    ls, hs, rows, lanes = out.shape
    half = mine.shape[0] // 2
    own = (mine[:half] + got[half:].astype(f32)).astype(bf16)
    other = (mine[half:] + got[:half].astype(f32)).astype(bf16)
    f = lanes // 2
    for h in range(hs):
        cols = slice(h * f, (h + 1) * f)
        both = jnp.concatenate([own[:, cols], other[:, cols]], axis=1)
        out[:, h] = both.reshape(ls, rows, lanes)


def sum_kernel(core, got, out):
    ls, hs, rows, lanes = got.shape
    total = got[:, 0].astype(f32)
    for h in range(1, hs):
        total = total + got[:, h].astype(f32)
    total = total.astype(bf16).reshape(ls * rows, lanes)
    perm = swap_matrix(ls, rows // 2)
    out[...] = dot(perm, total, ((1,), (0,))).astype(bf16).reshape(out.shape)


def token_kernel(core, eid, slot, got, out):
    quarters, f = out.shape[0], out.shape[1]
    xs = got.shape[0] // quarters
    rows = xs * got.shape[1]
    first = slot_onehot(eid[...], slot[...], core[0], rows).astype(f32).astype(bf16)
    second = slot_onehot(eid[...], slot[...], 1 - core[0], rows).astype(f32).astype(bf16)
    for q in range(quarters):
        table = got[q * xs : (q + 1) * xs].reshape(rows, 2 * f)
        low = dot(table, first, ((0,), (0,)))
        high = dot(table, second, ((0,), (0,)))
        out[q] = (low[:f] + high[f:]).astype(bf16)


def grads_kernel(core, own, other, dh, act, g_in, g_out):
    half = dh.shape[0] // 2
    x = jnp.concatenate([own[:, 0].reshape(half, -1), other[:, 0].reshape(half, -1)], axis=0)
    g_in[...] = dot(x, dh[...], ((0,), (0,))).astype(bf16)
    dy = jnp.concatenate([own[:, 1].reshape(half, -1), other[:, 1].reshape(half, -1)], axis=0)
    g_out[...] = dot(act[...], dy, ((0,), (0,))).astype(bf16)


def exchange(x, axes):
    return lax.all_to_all(x, axes, split_axis=0, concat_axis=0, tiled=True)


def other_core(x):
    return lax.ppermute(x, "c", [(0, 1), (1, 0)])


def local(tokens, cotangent, gate_value, expert_id, token_slot, w_in, w_out):
    ys, xs, ls, hs = (lax.axis_size(a) for a in ("y", "x", "l", "h"))
    width, hid = w_in.shape[1:]
    toks = tokens.shape[0]
    w_in, w_out = w_in[0], w_out[0]
    eid, slot, gate = (a.reshape(1, toks) for a in (expert_id, token_slot, gate_value))
    yx, rows = ys * xs, ys * xs * ls * 4
    (sent,) = call(dispatch_kernel, [((yx, 2, ls * 2, width), bf16)], eid, slot, gate, tokens, cotangent)
    got = exchange(sent, ("y", "x"))
    (sent,) = call(regroup_kernel, [((ls, 2, yx * 2, width), bf16)], got)
    own = exchange(sent, "l")
    other = other_core(own)
    (parts,) = call(parts_kernel, [((rows, 2 * hid), bf16)], own, other, w_in, w_out)
    got = exchange(parts.reshape(ys, rows // ys, 2 * hid), "y")
    dh, act = call(gelu_kernel, [((ys, rows // ys, hid), bf16)] * 2, got)
    dh = exchange(dh, "y").reshape(rows, hid)
    act = exchange(act, "y").reshape(rows, hid)
    mine, theirs = call(back_kernel, [((rows, width // 2), f32), ((rows, width // 2), bf16)], dh, w_in)
    got = other_core(theirs)
    f = width // 8
    (sent,) = call(pack_kernel, [((ls, hs, yx * 2, 2 * f), bf16)], mine, got)
    sent = sent.reshape(ls * hs, yx * 2, 2 * f)
    got = exchange(sent, ("l", "h")).reshape(ls, hs, yx * 2, 2 * f)
    g_in, g_out = call(grads_kernel, [((width, hid), bf16), ((hid, width), bf16)], own, other, dh, act)
    (sent,) = call(sum_kernel, [((yx, ls * 2, 2 * f), bf16)], got)
    got = exchange(sent, ("y", "x"))
    (grad_t,) = call(token_kernel, [((ys, f, toks), bf16)], eid, slot, got)
    return jnp.transpose(grad_t, (2, 0, 1)), g_in[None], g_out[None]


def solution(mesh):
    dp, expert, mp = mesh.devices.shape
    fine = Mesh(mesh.devices.reshape(dp, 4, expert // 4, mp // 2, 2), ("y", "x", "l", "h", "c"))
    group, ffn = ("y", "x", "l"), ("h", "c")
    in_specs = (
        P(group, None),
        P(group, None),
        P(group),
        P(group),
        P(group),
        P(("x", "l"), "y", ffn),
        P(("x", "l"), ffn, "y"),
    )
    out_specs = (P(group, None, ffn), P(("x", "l"), "y", ffn), P(("x", "l"), ffn, "y"))
    return jax.shard_map(local, mesh=fine, in_specs=in_specs, out_specs=out_specs, check_vma=False)
```

```python
import jax
import jax.numpy as jnp
from jax import lax
from jax.experimental import pallas as pl
from jax.experimental.pallas import tpu as pltpu
from jax.sharding import Mesh, PartitionSpec as P

tanh_scale = 0.7978845608028654
cubic_coef = 0.044715
f32 = jnp.float32
bf16 = jnp.bfloat16


def gelu_pair(pre_act):
    tanh_arg = tanh_scale * (pre_act + cubic_coef * pre_act * pre_act * pre_act)
    tanh_val = jnp.tanh(tanh_arg)
    gelu_value = 0.5 * pre_act * (1.0 + tanh_val)
    gelu_slope = 0.5 * (1.0 + tanh_val) + 0.5 * pre_act * (
        1.0 - tanh_val * tanh_val
    ) * tanh_scale * (1.0 + 3.0 * cubic_coef * pre_act * pre_act)
    return (gelu_value, gelu_slope)


def dot(a, b, dims):
    return lax.dot_general(a, b, ((dims[0], dims[1]), ((), ())), preferred_element_type=f32)


def size(shape):
    n = 1
    for s in shape:
        n *= s
    return n


def call(kernel, outs, *args, scratch=(), fetch=False, after=()):
    moved = sum(a.size * a.dtype.itemsize for a in args) + sum(
        jnp.dtype(d).itemsize * size(s) for s, d in outs
    )
    place = lax.axis_index(("h", "c")).astype(jnp.int32).reshape(1)
    space = pltpu.HBM if fetch else pltpu.VMEM
    return pl.pallas_call(
        kernel,
        out_shape=[jax.ShapeDtypeStruct(s, d) for s, d in outs],
        in_specs=[pl.BlockSpec(memory_space=pltpu.SMEM)]
        + [pl.BlockSpec(memory_space=space)] * len(args)
        + [pl.BlockSpec(memory_space=pl.ANY)] * len(after),
        out_specs=[pl.BlockSpec(memory_space=pltpu.VMEM)] * len(outs),
        scratch_shapes=scratch,
        compiler_params=pltpu.CompilerParams(vmem_limit_bytes=(60 if fetch else 32) * 1024 * 1024),
        cost_estimate=pl.CostEstimate(flops=0, bytes_accessed=moved, transcendentals=0),
    )(place, *args, *after)


def core(place):
    return place[0] & 1


def as_bf16(mask):
    return mask.astype(f32).astype(bf16)


def dispatch_kernel(place, eid, slot, gate, tok, cot, out, eid_v, slot_v, gate_v, tok_v, cot_v, sems):
    quarters, toks, feats = tok_v.shape
    count = out.shape[0] // quarters
    copies = [
        pltpu.make_async_copy(src, dst, sems.at[i])
        for i, (src, dst) in enumerate(((eid, eid_v), (slot, slot_v), (gate, gate_v)))
    ]
    for src, dst in ((tok, tok_v), (cot, cot_v)):
        for q in range(quarters):
            cols = pl.ds(pl.multiple_of((2 * q + core(place)) * feats, feats), feats)
            copies.append(pltpu.make_async_copy(src.at[:, cols], dst.at[q], sems.at[len(copies)]))
    for copy in copies:
        copy.start()
    for copy in copies[:3]:
        copy.wait()
    row = lax.broadcasted_iota(jnp.int32, (count, toks), 0)
    hit = (row // 8 == eid_v[...]) & (row % 4 == slot_v[...])
    is_x = row % 8 < 4
    take_x = as_bf16(hit & is_x)
    take_dy = as_bf16(hit & ~is_x)
    row_gate = jnp.sum(jnp.where(hit, gate_v[...], 0.0), axis=1, keepdims=True)
    for copy in copies[3:]:
        copy.wait()
    for q in range(quarters):
        got_x = dot(take_x, tok_v[q], ((1,), (0,)))
        got_dy = row_gate * dot(take_dy, cot_v[q], ((1,), (0,)))
        out[q * count : (q + 1) * count] = (got_x + got_dy).astype(bf16)


def regroup_kernel(place, got, out):
    ys, xs = 4, 4
    count = got.shape[0] // ys
    ls = count // (8 * xs)
    n = lax.broadcasted_iota(jnp.int32, (count, count), 0)
    col = lax.broadcasted_iota(jnp.int32, (count, count), 1)
    part = 2 * xs * ls
    low, x, at_l, s_hi, which = (
        n % 2,
        (n // 2) % xs,
        (n // (2 * xs)) % ls,
        (n // part) % 2,
        n // (2 * part),
    )
    perm = as_bf16(col == ((x * ls + at_l) * 2 + which) * 4 + s_hi * 2 + low)
    rows = [dot(perm, got[y * count : (y + 1) * count], ((1,), (0,))) for y in range(ys)]
    width = 2 * xs
    for which in range(2):
        for s_hi in range(2):
            for at_l in range(ls):
                source = slice(
                    which * 2 * part + s_hi * part + at_l * width,
                    which * 2 * part + s_hi * part + (at_l + 1) * width,
                )
                for y in range(0, ys, 2):
                    both = jnp.concatenate([rows[y][source], rows[y + 1][source]], axis=0)
                    at = (s_hi * ls + at_l) * ys * width + y * width
                    out[which, at : at + 2 * width] = both.astype(bf16)


def swap_matrix(outer, inner):
    n = outer * inner * 2
    row = lax.broadcasted_iota(jnp.int32, (n, n), 0)
    col = lax.broadcasted_iota(jnp.int32, (n, n), 1)
    pair = row // 2
    source = ((pair % outer) * inner + pair // outer) * 2 + row % 2
    return as_bf16(source == col)


def halves(place, ref, axis):
    n = ref.shape[axis] // 2
    for c in (core(place), 1 - core(place)):
        part = pl.ds(pl.multiple_of(c * n, n), n)
        yield ref[part, :] if axis == 0 else ref[:, part]


def parts_kernel(place, own, other, w_in, w_out, out):
    hid = w_in.shape[1]
    (in_own, in_other), (out_own, out_other) = halves(place, w_in, 0), halves(place, w_out, 1)
    out[:, :hid] = (
        dot(own[0], in_own, ((1,), (0,))) + dot(other[0], in_other, ((1,), (0,)))
    ).astype(bf16)
    out[:, hid:] = (
        dot(own[1], out_own, ((1,), (1,))) + dot(other[1], out_other, ((1,), (1,)))
    ).astype(bf16)


def gelu_kernel(place, got, dh, act):
    hid = dh.shape[2]
    total = got[0].astype(f32)
    for q in range(1, got.shape[0]):
        total = total + got[q].astype(f32)
    gelu_value, gelu_slope = gelu_pair(total[:, :hid])
    d_hidden = (total[:, hid:] * gelu_slope).astype(bf16)
    for q in range(got.shape[0]):
        dh[q] = d_hidden
    act[...] = gelu_value.astype(bf16)


def back_kernel(place, dh, w_in, mine, theirs):
    hs, block = 4, w_in.shape[0] // 8
    for out, c in ((theirs, 1 - core(place)), (mine, core(place))):
        w = jnp.concatenate(
            [
                w_in[pl.ds(pl.multiple_of(h * 2 * block + c * block, block), block), :]
                for h in range(hs)
            ],
            axis=0,
        )
        out[...] = dot(dh[...], w, ((1,), (1,))).astype(out.dtype)


def pack_kernel(place, mine, got, act, send_p, send_q, keep, acts, total):
    for q in range(acts.shape[0]):
        acts[q] = act[...]
    _, hs, rows, lanes = total.shape
    half, f, h = mine.shape[0] // 2, lanes // 2, place[0] >> 1
    both = mine[...] + got[...].astype(f32)
    for at in range(hs):
        cols = slice(at * f, (at + 1) * f)
        packed = jnp.concatenate([both[:half, cols], both[half:, cols]], axis=1)
        for stream in range(2):
            total[stream, at] = packed[stream * rows : (stream + 1) * rows]
    near, far = h ^ 1, 3 - h
    send_p[0] = total[0, near].astype(bf16)
    send_p[1] = total[0, 3 - near].astype(bf16)
    send_q[0] = total[1, far].astype(bf16)
    send_q[1] = total[1, far ^ 1].astype(bf16)
    keep[0, 0] = total[0, h]
    keep[0, 1] = total[0, far]
    keep[1, 0] = total[1, h]
    keep[1, 1] = total[1, near]


def halve_kernel(place, keep, got_p, got_q, _, send_p, send_q, left):
    for stream, got, send in ((0, got_p, send_p), (1, got_q, send_q)):
        send[...] = (keep[stream, 1] + got[1].astype(f32)).astype(bf16)
        left[stream] = keep[stream, 0] + got[0].astype(f32)


def final_kernel(place, left, got_p, got_q, out):
    rows = left.shape[1]
    out[:rows] = (left[0] + got_p[...].astype(f32)).astype(bf16)
    out[rows:] = (left[1] + got_q[...].astype(f32)).astype(bf16)


def turn_kernel(place, got, out):
    yx, inner, lanes = out.shape
    perm = swap_matrix(inner // 2, yx)
    out[...] = dot(perm, got[...], ((1,), (0,))).astype(bf16).reshape(out.shape)


def token_kernel(place, eid, slot, got, out):
    quarters, f, toks = out.shape
    xs = got.shape[0] // quarters
    rows = xs * got.shape[1]
    row = lax.broadcasted_iota(jnp.int32, (rows, toks), 0)
    mine = row // 2 == eid[...]
    first = as_bf16(mine & (row % 2 == slot[...]))
    second = as_bf16(mine & (row % 2 == slot[...] - 2))
    for q in range(quarters):
        table = got[q * xs : (q + 1) * xs].reshape(rows, 2 * f)
        low = dot(table, first, ((0,), (0,)))
        high = dot(table, second, ((0,), (0,)))
        out[q] = (low[:f] + high[f:]).astype(bf16)


def grads_kernel(place, own, other, dh, act, g_in, g_out):
    n = own.shape[2]
    for src, c in ((own, core(place)), (other, 1 - core(place))):
        part = pl.ds(pl.multiple_of(c * n, n), n)
        g_in[part, :] = dot(src[0], dh[...], ((0,), (0,))).astype(bf16)
        g_out[:, part] = dot(act[...], src[1], ((0,), (0,))).astype(bf16)


def exchange(x, axes):
    return lax.all_to_all(x, axes, split_axis=0, concat_axis=0, tiled=True)


def other_core(x):
    return lax.ppermute(x, "c", [(0, 1), (1, 0)])


def over_h(x, pairing):
    return lax.ppermute(x, "h", [(h, pairing(h)) for h in range(4)])


def local(tokens, cotangent, gate_value, expert_id, token_slot, w_in, w_out):
    ys, xs, ls = (lax.axis_size(a) for a in ("y", "x", "l"))
    width, hid = w_in.shape[1:]
    toks = tokens.shape[0]
    w_in, w_out = w_in[0], w_out[0]
    eid, slot, gate = (a.reshape(1, toks) for a in (expert_id, token_slot, gate_value))
    yx, groups = ys * xs, ys * xs * ls
    rows, part, f = groups * 4, width // 2, width // 8
    near, far = (lambda h: h ^ 1), (lambda h: 3 - h)
    (sent,) = call(
        dispatch_kernel,
        [((groups * 8, part), bf16)],
        eid,
        slot,
        gate,
        tokens,
        cotangent,
        scratch=[
            pltpu.VMEM((1, toks), jnp.int32),
            pltpu.VMEM((1, toks), jnp.int32),
            pltpu.VMEM((1, toks), f32),
            pltpu.VMEM((ys, toks, part), bf16),
            pltpu.VMEM((ys, toks, part), bf16),
            pltpu.SemaphoreType.DMA((3 + 2 * ys,)),
        ],
        fetch=True,
    )
    got = exchange(sent.reshape(groups, 8, part), ("y", "x", "l")).reshape(groups * 8, part)
    (own,) = call(regroup_kernel, [((2, rows, part), bf16)], got)
    other = other_core(own)
    (parts,) = call(parts_kernel, [((rows, 2 * hid), bf16)], own, other, w_in, w_out)
    got = exchange(parts.reshape(ys, rows // ys, 2 * hid), "y")
    block = (rows // ys, hid)
    dh, act = call(gelu_kernel, [((ys,) + block, bf16), (block, bf16)], got)
    dh = exchange(dh, "y").reshape(rows, hid)
    mine, theirs = call(back_kernel, [((rows, part), f32), ((rows, part), bf16)], dh, w_in)
    got = other_core(theirs)
    tile = (rows // 4, 2 * f)
    send_p, send_q, keep, acts = call(
        pack_kernel,
        [((2,) + tile, bf16), ((2,) + tile, bf16), ((2, 2) + tile, f32), ((ys,) + block, bf16)],
        mine,
        got,
        act,
        scratch=[pltpu.VMEM((2, 4) + tile, f32)],
    )
    got_p, got_q = over_h(send_p, near), over_h(send_q, far)
    act = exchange(acts, "y").reshape(rows, hid)
    send_p, send_q, left = call(
        halve_kernel,
        [(tile, bf16), (tile, bf16), ((2,) + tile, f32)],
        keep,
        got_p,
        got_q,
        after=(act,),
    )
    got_p, got_q = over_h(send_p, far), over_h(send_q, near)
    (sent,) = call(final_kernel, [((rows // 2, 2 * f), bf16)], left, got_p, got_q)
    got = exchange(sent.reshape(ls, yx * 2, 2 * f), "l").reshape(rows // 2, 2 * f)
    (sent,) = call(turn_kernel, [((yx, ls * 2, 2 * f), bf16)], got)
    got = exchange(sent, ("y", "x"))
    g_in, g_out = call(grads_kernel, [((width, hid), bf16), ((hid, width), bf16)], own, other, dh, act)
    (grad_t,) = call(token_kernel, [((ys, f, toks), bf16)], eid, slot, got)
    return jnp.transpose(grad_t, (2, 0, 1)), g_in[None], g_out[None]


def solution(mesh):
    dp, expert, mp = mesh.devices.shape
    fine = Mesh(mesh.devices.reshape(dp, 4, expert // 4, mp // 2, 2), ("y", "x", "l", "h", "c"))
    group, ffn = ("y", "x", "l"), ("h", "c")
    in_specs = (
        P(group, None),
        P(group, None),
        P(group),
        P(group),
        P(group),
        P(("x", "l"), "y", ffn),
        P(("x", "l"), ffn, "y"),
    )
    out_specs = (P(group, None, ffn), P(("x", "l"), "y", ffn), P(("x", "l"), ffn, "y"))
    return jax.shard_map(local, mesh=fine, in_specs=in_specs, out_specs=out_specs, check_vma=False)
```

```python
import jax
import jax.numpy as jnp
from jax import lax
from jax.experimental import pallas as pl
from jax.experimental.pallas import tpu as pltpu
from jax.sharding import Mesh, PartitionSpec as P

tanh_scale = 0.7978845608028654
cubic_coef = 0.044715
f32 = jnp.float32
bf16 = jnp.bfloat16


def gelu_pair(pre_act):
    tanh_arg = tanh_scale * (pre_act + cubic_coef * pre_act * pre_act * pre_act)
    tanh_val = jnp.tanh(tanh_arg)
    gelu_value = 0.5 * pre_act * (1.0 + tanh_val)
    gelu_slope = 0.5 * (1.0 + tanh_val) + 0.5 * pre_act * (
        1.0 - tanh_val * tanh_val
    ) * tanh_scale * (1.0 + 3.0 * cubic_coef * pre_act * pre_act)
    return (gelu_value, gelu_slope)


def dot(a, b, dims):
    return lax.dot_general(a, b, ((dims[0], dims[1]), ((), ())), preferred_element_type=f32)


def size(shape):
    n = 1
    for s in shape:
        n *= s
    return n


def call(kernel, outs, *args, scratch=(), fetch=False, after=(), passed=()):
    moved = sum(a.size * a.dtype.itemsize for a in args) + sum(
        jnp.dtype(d).itemsize * size(s) for s, d in outs
    )
    place = (lax.axis_index("y") * 2 + lax.axis_index("c")).astype(jnp.int32).reshape(1)
    space = pltpu.HBM if fetch else pltpu.VMEM
    return pl.pallas_call(
        kernel,
        out_shape=[jax.ShapeDtypeStruct(s, d) for s, d in outs],
        in_specs=[pl.BlockSpec(memory_space=pltpu.SMEM)]
        + [pl.BlockSpec(memory_space=space)] * len(args)
        + [pl.BlockSpec(memory_space=pl.ANY)] * len(after),
        out_specs=[pl.BlockSpec(memory_space=pltpu.VMEM)] * (len(outs) - len(passed))
        + [pl.BlockSpec(memory_space=pltpu.HBM)] * len(passed),
        scratch_shapes=scratch,
        compiler_params=pltpu.CompilerParams(vmem_limit_bytes=(60 if fetch else 16) * 1024 * 1024),
        cost_estimate=pl.CostEstimate(flops=0, bytes_accessed=moved, transcendentals=0),
    )(place, *args, *after)


def core(place):
    return place[0] & 1


def as_bf16(mask):
    return mask.astype(f32).astype(bf16)


def dispatch_kernel(
    place, eid, slot, gate, tok, cot, w_in, out, w_pass, eid_v, slot_v, gate_v, tok_v, cot_v, sems
):
    quarters, toks, feats = tok_v.shape
    count = out.shape[0] // quarters
    copies = [
        pltpu.make_async_copy(src, dst, sems.at[i])
        for i, (src, dst) in enumerate(((eid, eid_v), (slot, slot_v), (gate, gate_v)))
    ]
    for src, dst in ((tok, tok_v), (cot, cot_v)):
        for q in range(quarters):
            cols = pl.ds(pl.multiple_of((2 * q + core(place)) * feats, feats), feats)
            copies.append(pltpu.make_async_copy(src.at[:, cols], dst.at[q], sems.at[len(copies)]))
    copies.append(pltpu.make_async_copy(w_in, w_pass, sems.at[len(copies)]))
    for copy in copies:
        copy.start()
    for copy in copies[:3]:
        copy.wait()
    row = lax.broadcasted_iota(jnp.int32, (count, toks), 0)
    hit = (row // 8 == eid_v[...]) & (row % 4 == slot_v[...])
    is_x = row % 8 < 4
    take_x = as_bf16(hit & is_x)
    take_dy = as_bf16(hit & ~is_x)
    row_gate = jnp.sum(jnp.where(hit, gate_v[...], 0.0), axis=1, keepdims=True)
    for copy in copies[3:-1]:
        copy.wait()
    for q in range(quarters):
        got_x = dot(take_x, tok_v[q], ((1,), (0,)))
        got_dy = row_gate * dot(take_dy, cot_v[q], ((1,), (0,)))
        out[q * count : (q + 1) * count] = (got_x + got_dy).astype(bf16)
    copies[-1].wait()


def regroup_kernel(place, got, _, __, out):
    rows = out.shape[1] // 4
    count = 2 * rows
    n = lax.broadcasted_iota(jnp.int32, (count, count), 0)
    col = lax.broadcasted_iota(jnp.int32, (count, count), 1)
    which, group, slot = n // rows, (n % rows) // 4, n % 4
    perm = as_bf16(col == group * 8 + which * 4 + slot)
    for y in range(4):
        moved = dot(perm, got[y * count : (y + 1) * count], ((1,), (0,))).astype(bf16)
        out[0, y * rows : (y + 1) * rows] = moved[:rows]
        out[1, y * rows : (y + 1) * rows] = moved[rows:]


def arrange_kernel(place, own, left, right, far_low, far_high, mine, theirs):
    y, c = place[0] >> 1, core(place)
    hs = 4
    f = own.shape[0] // (2 * hs)
    for out, at in ((mine, c), (theirs, 1 - c)):
        for src, q in ((own, y), (left, (y + 3) & 3), (right, (y + 1) & 3), (None, (y + 2) & 3)):
            for h in range(hs):
                ref, h_in = (src, h) if src is not None else ((far_low, far_high)[h // 2], h % 2)
                rows = ref[pl.ds(pl.multiple_of((h_in * 2 + at) * f, f), f), :]
                out[pl.ds(pl.multiple_of((h * 4 + q) * f, f), f), :] = rows


def halves(place, ref, axis):
    n = ref.shape[axis] // 2
    for c in (core(place), 1 - core(place)):
        part = pl.ds(pl.multiple_of(c * n, n), n)
        yield ref[part, :] if axis == 0 else ref[:, part]


def parts_kernel(place, own, other, w_in, w_out, out):
    hid = w_in.shape[1]
    (in_own, in_other), (out_own, out_other) = halves(place, w_in, 0), halves(place, w_out, 1)
    out[:, :hid] = (
        dot(own[0], in_own, ((1,), (0,))) + dot(other[0], in_other, ((1,), (0,)))
    ).astype(bf16)
    out[:, hid:] = (
        dot(own[1], out_own, ((1,), (1,))) + dot(other[1], out_other, ((1,), (1,)))
    ).astype(bf16)


def gelu_kernel(place, got, both):
    hid = both.shape[1] // 2
    total = got[0].astype(f32)
    for q in range(1, got.shape[0]):
        total = total + got[q].astype(f32)
    gelu_value, gelu_slope = gelu_pair(total[:, :hid])
    both[:, :hid] = (total[:, hid:] * gelu_slope).astype(bf16)
    both[:, hid:] = gelu_value.astype(bf16)


def back_kernel(place, both, w_mine, w_theirs, mine, theirs):
    d_hidden = both[:, : both.shape[1] // 2]
    theirs[...] = dot(d_hidden, w_theirs[...], ((1,), (1,))).astype(bf16)
    mine[...] = dot(d_hidden, w_mine[...], ((1,), (1,)))


def pack_kernel(place, mine, got, out):
    n = out.shape[2]
    for h in range(out.shape[0]):
        cols = slice(h * n, (h + 1) * n)
        out[h] = (mine[:, cols] + got[:, cols].astype(f32)).astype(bf16)


def sum_kernel(place, got, out):
    total = got[0].astype(f32)
    for h in range(1, got.shape[0]):
        total = total + got[h].astype(f32)
    total = total.astype(bf16)
    rows, lanes = out.shape
    row = lax.broadcasted_iota(jnp.int32, (rows, total.shape[0]), 0)
    col = lax.broadcasted_iota(jnp.int32, (rows, total.shape[0]), 1)
    source = (row // 8) * 4 + row % 4
    moved = 0.0
    for q_hi in range(2):
        take = as_bf16((source == col) & ((row // 4) % 2 == q_hi))
        moved = moved + dot(take, total[:, q_hi * lanes : (q_hi + 1) * lanes], ((1,), (0,)))
    out[...] = moved.astype(bf16)


def token_kernel(place, eid, slot, got, out):
    quarters, f, toks = out.shape
    row = lax.broadcasted_iota(jnp.int32, (got.shape[0], toks), 0)
    hit = (row // 8 == eid[...]) & (row % 4 == slot[...])
    for q_hi in range(quarters // 2):
        take = as_bf16(hit & ((row // 4) % 2 == q_hi))
        picked = dot(got[...], take, ((0,), (0,))).astype(bf16)
        out[2 * q_hi] = picked[:f]
        out[2 * q_hi + 1] = picked[f:]


def grads_kernel(place, own, other, both, g_in, g_out):
    n, hid = own.shape[2], both.shape[1] // 2
    for src, c in ((own, core(place)), (other, 1 - core(place))):
        part = pl.ds(pl.multiple_of(c * n, n), n)
        g_in[part, :] = dot(src[0], both[:, :hid], ((0,), (0,))).astype(bf16)
        g_out[:, part] = dot(both[:, hid:], src[1], ((0,), (0,))).astype(bf16)


def exchange(x, axes):
    return lax.all_to_all(x, axes, split_axis=0, concat_axis=0, tiled=True)


def other_core(x):
    return lax.ppermute(x, "c", [(0, 1), (1, 0)])


def over_y(x, step):
    return lax.ppermute(x, "y", [(y, (y + step) % 4) for y in range(4)])


def local(tokens, cotangent, gate_value, expert_id, token_slot, w_in, w_out):
    ys, xs, ls, hs = (lax.axis_size(a) for a in ("y", "x", "l", "h"))
    width, hid = w_in.shape[1:]
    toks = tokens.shape[0]
    w_in, w_out = w_in[0], w_out[0]
    eid, slot, gate = (a.reshape(1, toks) for a in (expert_id, token_slot, gate_value))
    groups = ys * xs * ls
    rows, part, f = groups * 4, width // 2, width // 8
    chunk = rows // ys
    sent, w_pass = call(
        dispatch_kernel,
        [((groups * 8, part), bf16), (w_in.shape, bf16)],
        eid,
        slot,
        gate,
        tokens,
        cotangent,
        w_in,
        scratch=[
            pltpu.VMEM((1, toks), jnp.int32),
            pltpu.VMEM((1, toks), jnp.int32),
            pltpu.VMEM((1, toks), f32),
            pltpu.VMEM((ys, toks, part), bf16),
            pltpu.VMEM((ys, toks, part), bf16),
            pltpu.SemaphoreType.DMA((4 + 2 * ys,)),
        ],
        fetch=True,
        passed=(1,),
    )
    got = exchange(sent.reshape(groups, 8, part), ("y", "x", "l")).reshape(groups * 8, part)
    left, right = over_y(w_pass, 1), over_y(w_pass, -1)
    far_low, far_high = over_y(right[:part], -1), over_y(left[part:], 1)
    w_mine, w_theirs = call(
        arrange_kernel, [((ys * part, hid), bf16)] * 2, w_pass, left, right, far_low, far_high
    )
    (own,) = call(regroup_kernel, [((2, rows, part), bf16)], got, after=(w_mine, w_theirs))
    other = other_core(own)
    (parts,) = call(parts_kernel, [((rows, 2 * hid), bf16)], own, other, w_in, w_out)
    got = exchange(parts.reshape(ys, chunk, 2 * hid), "y")
    (both,) = call(gelu_kernel, [((chunk, 2 * hid), bf16)], got)
    mine, theirs = call(
        back_kernel, [((chunk, ys * part), f32), ((chunk, ys * part), bf16)], both, w_mine, w_theirs
    )
    got = other_core(theirs)
    (sent,) = call(pack_kernel, [((hs, chunk, part), bf16)], mine, got)
    got = exchange(sent, "h")
    (sent,) = call(sum_kernel, [((xs * ls * 8, 2 * f), bf16)], got)
    got = exchange(sent.reshape(xs * ls, 8, 2 * f), ("x", "l")).reshape(xs * ls * 8, 2 * f)
    both = lax.all_gather(both, "y", axis=0, tiled=True)
    g_in, g_out = call(grads_kernel, [((width, hid), bf16), ((hid, width), bf16)], own, other, both)
    (grad_t,) = call(token_kernel, [((ys, f, toks), bf16)], eid, slot, got)
    return jnp.transpose(grad_t, (2, 0, 1)), g_in[None], g_out[None]


def solution(mesh):
    dp, expert, mp = mesh.devices.shape
    fine = Mesh(mesh.devices.reshape(dp, 4, expert // 4, mp // 2, 2), ("y", "x", "l", "h", "c"))
    group, ffn = ("y", "x", "l"), ("h", "c")
    in_specs = (
        P(group, None),
        P(group, None),
        P(group),
        P(group),
        P(group),
        P(("x", "l"), "y", ffn),
        P(("x", "l"), ffn, "y"),
    )
    out_specs = (P(group, None, ffn), P(("x", "l"), "y", ffn), P(("x", "l"), ffn, "y"))
    return jax.shard_map(local, mesh=fine, in_specs=in_specs, out_specs=out_specs, check_vma=False)
```

```python
import jax
import jax.numpy as jnp
from jax import lax
from jax.experimental import pallas as pl
from jax.experimental.pallas import tpu as pltpu
from jax.sharding import Mesh, PartitionSpec as P

tanh_scale = 0.7978845608028654
cubic_coef = 0.044715
f32 = jnp.float32
bf16 = jnp.bfloat16


def gelu_pair(pre_act):
    tanh_arg = tanh_scale * (pre_act + cubic_coef * pre_act * pre_act * pre_act)
    tanh_val = jnp.tanh(tanh_arg)
    gelu_value = 0.5 * pre_act * (1.0 + tanh_val)
    gelu_slope = 0.5 * (1.0 + tanh_val) + 0.5 * pre_act * (
        1.0 - tanh_val * tanh_val
    ) * tanh_scale * (1.0 + 3.0 * cubic_coef * pre_act * pre_act)
    return (gelu_value, gelu_slope)


def dot(a, b, dims):
    return lax.dot_general(a, b, ((dims[0], dims[1]), ((), ())), preferred_element_type=f32)


def size(shape):
    n = 1
    for s in shape:
        n *= s
    return n


def call(kernel, outs, *args, scratch=(), fetch=False, after=()):
    moved = sum(a.size * a.dtype.itemsize for a in args) + sum(
        jnp.dtype(d).itemsize * size(s) for s, d in outs
    )
    place = (lax.axis_index("y") * 2 + lax.axis_index("c")).astype(jnp.int32).reshape(1)
    space = pltpu.HBM if fetch else pltpu.VMEM
    return pl.pallas_call(
        kernel,
        out_shape=[jax.ShapeDtypeStruct(s, d) for s, d in outs],
        in_specs=[pl.BlockSpec(memory_space=pltpu.SMEM)]
        + [pl.BlockSpec(memory_space=space)] * len(args)
        + [pl.BlockSpec(memory_space=pl.ANY)] * len(after),
        out_specs=[pl.BlockSpec(memory_space=pltpu.VMEM)] * len(outs),
        scratch_shapes=scratch,
        compiler_params=pltpu.CompilerParams(vmem_limit_bytes=(60 if fetch else 16) * 1024 * 1024),
        cost_estimate=pl.CostEstimate(flops=0, bytes_accessed=moved, transcendentals=0),
    )(place, *args, *after)


def core(place):
    return place[0] & 1


def as_bf16(mask):
    return mask.astype(f32).astype(bf16)


def dispatch_kernel(
    place, eid, slot, gate, tok, cot, w_in, out, w_pass, eid_v, slot_v, gate_v, tok_v, cot_v, sems
):
    quarters, toks, feats = tok_v.shape
    count = out.shape[0] // quarters
    copies = [
        pltpu.make_async_copy(src, dst, sems.at[i])
        for i, (src, dst) in enumerate(((eid, eid_v), (slot, slot_v), (gate, gate_v)))
    ]
    for src, dst in ((tok, tok_v), (cot, cot_v)):
        for q in range(quarters):
            cols = pl.ds(pl.multiple_of((2 * q + core(place)) * feats, feats), feats)
            copies.append(pltpu.make_async_copy(src.at[:, cols], dst.at[q], sems.at[len(copies)]))
    copies.append(pltpu.make_async_copy(w_in, w_pass, sems.at[len(copies)]))
    for copy in copies:
        copy.start()
    for copy in copies[:3]:
        copy.wait()
    row = lax.broadcasted_iota(jnp.int32, (count, toks), 0)
    hit = (row // 8 == eid_v[...]) & (row % 4 == slot_v[...])
    is_x = row % 8 < 4
    take_x = as_bf16(hit & is_x)
    take_dy = as_bf16(hit & ~is_x)
    row_gate = jnp.sum(jnp.where(hit, gate_v[...], 0.0), axis=1, keepdims=True)
    for copy in copies[3:-1]:
        copy.wait()
    for q in range(quarters):
        got_x = dot(take_x, tok_v[q], ((1,), (0,)))
        got_dy = row_gate * dot(take_dy, cot_v[q], ((1,), (0,)))
        out[q * count : (q + 1) * count] = (got_x + got_dy).astype(bf16)
    copies[-1].wait()


def regroup_kernel(place, got, _, out):
    rows, xs = out.shape[1] // 4, 4
    count = 2 * rows
    n = lax.broadcasted_iota(jnp.int32, (count, count), 0)
    col = lax.broadcasted_iota(jnp.int32, (count, count), 1)
    which, at_l, x, slot = n // rows, (n % rows) // (4 * xs), (n // 4) % xs, n % 4
    perm = as_bf16(col == ((x * (rows // (4 * xs)) + at_l) * 2 + which) * 4 + slot)
    for y in range(4):
        moved = dot(perm, got[y * count : (y + 1) * count], ((1,), (0,))).astype(bf16)
        out[0, y * rows : (y + 1) * rows] = moved[:rows]
        out[1, y * rows : (y + 1) * rows] = moved[rows:]


def arrange_kernel(place, own, left, right, far_low, far_high, mine, theirs, done):
    done[...] = jnp.zeros_like(done)
    y, c = place[0] >> 1, core(place)
    hs = 4
    f = own.shape[0] // (2 * hs)
    for out, at in ((mine, c), (theirs, 1 - c)):
        for src, q in ((own, y), (left, (y + 3) & 3), (right, (y + 1) & 3), (None, (y + 2) & 3)):
            for h in range(hs):
                ref, h_in = (src, h) if src is not None else ((far_low, far_high)[h // 2], h % 2)
                rows = ref[pl.ds(pl.multiple_of((h_in * 2 + at) * f, f), f), :]
                out[pl.ds(pl.multiple_of((h * 4 + q) * f, f), f), :] = rows


def halves(place, ref, axis):
    n = ref.shape[axis] // 2
    for c in (core(place), 1 - core(place)):
        part = pl.ds(pl.multiple_of(c * n, n), n)
        yield ref[part, :] if axis == 0 else ref[:, part]


def parts_kernel(place, own, other, w_in, w_out, out):
    hid = w_in.shape[1]
    (in_own, in_other), (out_own, out_other) = halves(place, w_in, 0), halves(place, w_out, 1)
    out[:, :hid] = (
        dot(own[0], in_own, ((1,), (0,))) + dot(other[0], in_other, ((1,), (0,)))
    ).astype(bf16)
    out[:, hid:] = (
        dot(own[1], out_own, ((1,), (1,))) + dot(other[1], out_other, ((1,), (1,)))
    ).astype(bf16)


def gelu_kernel(place, got, dh, act):
    hid = dh.shape[1]
    total = got[0].astype(f32)
    for q in range(1, got.shape[0]):
        total = total + got[q].astype(f32)
    gelu_value, gelu_slope = gelu_pair(total[:, :hid])
    dh[...] = (total[:, hid:] * gelu_slope).astype(bf16)
    act[...] = gelu_value.astype(bf16)


def back_kernel(place, dh, w_mine, w_theirs, mine, theirs):
    theirs[...] = dot(dh[...], w_theirs[...], ((1,), (1,))).astype(bf16)
    mine[...] = dot(dh[...], w_mine[...], ((1,), (1,)))


def pack_kernel(place, mine, got, out):
    ls, hs, rows, n = out.shape
    for h in range(hs):
        cols = slice(h * n, (h + 1) * n)
        both = (mine[:, cols] + got[:, cols].astype(f32)).astype(bf16)
        out[:, h] = both.reshape(ls, rows, n)


def sum_kernel(place, got, _, out):
    ls, hs, inner, n = got.shape
    total = got[:, 0].astype(f32)
    for h in range(1, hs):
        total = total + got[:, h].astype(f32)
    rows = ls * inner
    row = lax.broadcasted_iota(jnp.int32, (rows, rows), 0)
    col = lax.broadcasted_iota(jnp.int32, (rows, rows), 1)
    perm = as_bf16(col == (row // 4) % ls * inner + row // (4 * ls) * 4 + row % 4)
    out[...] = dot(perm, total.astype(bf16).reshape(rows, n), ((1,), (0,))).astype(bf16)


def token_kernel(place, eid, slot, got, out):
    quarters, f, toks = out.shape
    row = lax.broadcasted_iota(jnp.int32, (got.shape[0], toks), 0)
    take = as_bf16((row // 4 == eid[...]) & (row % 4 == slot[...]))
    picked = dot(got[...], take, ((0,), (0,))).astype(bf16)
    for q in range(quarters):
        out[q] = picked[q * f : (q + 1) * f]


def grads_kernel(place, own, other, dh, act, g_in, g_out, done):
    done[...] = jnp.zeros_like(done)
    n = own.shape[2]
    for src, c in ((own, core(place)), (other, 1 - core(place))):
        part = pl.ds(pl.multiple_of(c * n, n), n)
        g_in[part, :] = dot(src[0], dh[...], ((0,), (0,))).astype(bf16)
        g_out[:, part] = dot(act[...], src[1], ((0,), (0,))).astype(bf16)


def exchange(x, axes):
    return lax.all_to_all(x, axes, split_axis=0, concat_axis=0, tiled=True)


def other_core(x):
    return lax.ppermute(x, "c", [(0, 1), (1, 0)])


def over_y(x, step):
    return lax.ppermute(x, "y", [(y, (y + step) % 4) for y in range(4)])


def local(tokens, cotangent, gate_value, expert_id, token_slot, w_in, w_out):
    ys, xs, ls, hs = (lax.axis_size(a) for a in ("y", "x", "l", "h"))
    width, hid = w_in.shape[1:]
    toks = tokens.shape[0]
    w_in, w_out = w_in[0], w_out[0]
    eid, slot, gate = (a.reshape(1, toks) for a in (expert_id, token_slot, gate_value))
    groups = ys * xs * ls
    rows, part, f = groups * 4, width // 2, width // 8
    chunk = rows // ys
    sent, w_pass = call(
        dispatch_kernel,
        [((groups * 8, part), bf16), (w_in.shape, bf16)],
        eid,
        slot,
        gate,
        tokens,
        cotangent,
        w_in,
        scratch=[
            pltpu.VMEM((1, toks), jnp.int32),
            pltpu.VMEM((1, toks), jnp.int32),
            pltpu.VMEM((1, toks), f32),
            pltpu.VMEM((ys, toks, part), bf16),
            pltpu.VMEM((ys, toks, part), bf16),
            pltpu.SemaphoreType.DMA((4 + 2 * ys,)),
        ],
        fetch=True,
    )
    got = exchange(sent.reshape(groups, 8, part), ("y", "x", "l")).reshape(groups * 8, part)
    left, right = over_y(w_pass, 1), over_y(w_pass, -1)
    far_low, far_high = over_y(right[:part], -1), over_y(left[part:], 1)
    token = ((8, 128), f32)
    w_mine, w_theirs, done = call(
        arrange_kernel, [((ys * part, hid), bf16)] * 2 + [token], w_pass, left, right, far_low, far_high
    )
    (own,) = call(regroup_kernel, [((2, rows, part), bf16)], got, after=(done,))
    other = other_core(own)
    (parts,) = call(parts_kernel, [((rows, 2 * hid), bf16)], own, other, w_in, w_out)
    got = exchange(parts.reshape(ys, chunk, 2 * hid), "y")
    dh, act = call(gelu_kernel, [((chunk, hid), bf16)] * 2, got)
    mine, theirs = call(
        back_kernel, [((chunk, ys * part), f32), ((chunk, ys * part), bf16)], dh, w_mine, w_theirs
    )
    got = other_core(theirs)
    (sent,) = call(pack_kernel, [((ls, hs, xs * 4, part), bf16)], mine, got)
    got = exchange(sent.reshape(ls * hs, xs * 4, part), ("l", "h"))
    dh, act = (lax.all_gather(a, "y", axis=0, tiled=True) for a in (dh, act))
    g_in, g_out, done = call(
        grads_kernel, [((width, hid), bf16), ((hid, width), bf16), token], own, other, dh, act
    )
    (sent,) = call(
        sum_kernel, [((chunk, part), bf16)], got.reshape(ls, hs, xs * 4, part), after=(done,)
    )
    got = exchange(sent.reshape(xs, ls * 4, part), "x").reshape(chunk, part)
    (grad_t,) = call(token_kernel, [((ys, f, toks), bf16)], eid, slot, got)
    return jnp.transpose(grad_t, (2, 0, 1)), g_in[None], g_out[None]


def solution(mesh):
    dp, expert, mp = mesh.devices.shape
    fine = Mesh(mesh.devices.reshape(dp, 4, expert // 4, mp // 2, 2), ("y", "x", "l", "h", "c"))
    group, ffn = ("y", "x", "l"), ("h", "c")
    in_specs = (
        P(group, None),
        P(group, None),
        P(group),
        P(group),
        P(group),
        P(("x", "l"), "y", ffn),
        P(("x", "l"), ffn, "y"),
    )
    out_specs = (P(group, None, ffn), P(("x", "l"), "y", ffn), P(("x", "l"), ffn, "y"))
    return jax.shard_map(local, mesh=fine, in_specs=in_specs, out_specs=out_specs, check_vma=False)
```

```python
import jax
import jax.numpy as jnp
from jax import lax
from jax.experimental import pallas as pl
from jax.experimental.pallas import tpu as pltpu
from jax.sharding import Mesh, PartitionSpec as P

tanh_scale = 0.7978845608028654
cubic_coef = 0.044715
f32 = jnp.float32
bf16 = jnp.bfloat16


def gelu_pair(pre_act):
    tanh_arg = tanh_scale * (pre_act + cubic_coef * pre_act * pre_act * pre_act)
    tanh_val = jnp.tanh(tanh_arg)
    gelu_value = 0.5 * pre_act * (1.0 + tanh_val)
    gelu_slope = 0.5 * (1.0 + tanh_val) + 0.5 * pre_act * (
        1.0 - tanh_val * tanh_val
    ) * tanh_scale * (1.0 + 3.0 * cubic_coef * pre_act * pre_act)
    return (gelu_value, gelu_slope)


def dot(a, b, dims):
    return lax.dot_general(a, b, ((dims[0], dims[1]), ((), ())), preferred_element_type=f32)


def size(shape):
    n = 1
    for s in shape:
        n *= s
    return n


def call(kernel, outs, *args, scratch=(), fetch=False, after=()):
    moved = sum(a.size * a.dtype.itemsize for a in args) + sum(
        jnp.dtype(d).itemsize * size(s) for s, d in outs
    )
    place = (lax.axis_index("y") * 2 + lax.axis_index("c")).astype(jnp.int32).reshape(1)
    space = pltpu.HBM if fetch else pltpu.VMEM
    return pl.pallas_call(
        kernel,
        out_shape=[jax.ShapeDtypeStruct(s, d) for s, d in outs],
        in_specs=[pl.BlockSpec(memory_space=pltpu.SMEM)]
        + [pl.BlockSpec(memory_space=space)] * len(args)
        + [pl.BlockSpec(memory_space=pl.ANY)] * len(after),
        out_specs=[pl.BlockSpec(memory_space=pltpu.VMEM)] * len(outs),
        scratch_shapes=scratch,
        compiler_params=pltpu.CompilerParams(vmem_limit_bytes=(60 if fetch else 16) * 1024 * 1024),
        cost_estimate=pl.CostEstimate(flops=0, bytes_accessed=moved, transcendentals=0),
    )(place, *args, *after)


def core(place):
    return place[0] & 1


def as_bf16(mask):
    return mask.astype(f32).astype(bf16)


def dispatch_kernel(
    place, eid, slot, gate, tok, cot, w_in, out, w_pass, eid_v, slot_v, gate_v, tok_v, cot_v, sems
):
    quarters, toks, feats = tok_v.shape
    count = out.shape[0] // quarters
    copies = [
        pltpu.make_async_copy(src, dst, sems.at[i])
        for i, (src, dst) in enumerate(((eid, eid_v), (slot, slot_v), (gate, gate_v)))
    ]
    for src, dst in ((tok, tok_v), (cot, cot_v)):
        for q in range(quarters):
            cols = pl.ds(pl.multiple_of((2 * q + core(place)) * feats, feats), feats)
            copies.append(pltpu.make_async_copy(src.at[:, cols], dst.at[q], sems.at[len(copies)]))
    copies.append(pltpu.make_async_copy(w_in, w_pass, sems.at[len(copies)]))
    for copy in copies:
        copy.start()
    for copy in copies[:3]:
        copy.wait()
    row = lax.broadcasted_iota(jnp.int32, (count, toks), 0)
    hit = (row // 8 == eid_v[...]) & (row % 4 == slot_v[...])
    is_x = row % 8 < 4
    take_x = as_bf16(hit & is_x)
    take_dy = as_bf16(hit & ~is_x)
    row_gate = jnp.sum(jnp.where(hit, gate_v[...], 0.0), axis=1, keepdims=True)
    for copy in copies[3:-1]:
        copy.wait()
    for q in range(quarters):
        got_x = dot(take_x, tok_v[q], ((1,), (0,)))
        got_dy = row_gate * dot(take_dy, cot_v[q], ((1,), (0,)))
        out[q * count : (q + 1) * count] = (got_x + got_dy).astype(bf16)
    copies[-1].wait()


def regroup_kernel(place, got, _, __, out):
    rows, xs = out.shape[1] // 4, 4
    count = 2 * rows
    n = lax.broadcasted_iota(jnp.int32, (count, count), 0)
    col = lax.broadcasted_iota(jnp.int32, (count, count), 1)
    which, at_l, x, slot = n // rows, (n % rows) // (4 * xs), (n // 4) % xs, n % 4
    perm = as_bf16(col == ((x * (rows // (4 * xs)) + at_l) * 2 + which) * 4 + slot)
    for y in range(4):
        moved = dot(perm, got[y * count : (y + 1) * count], ((1,), (0,))).astype(bf16)
        out[0, y * rows : (y + 1) * rows] = moved[:rows]
        out[1, y * rows : (y + 1) * rows] = moved[rows:]


def halves(place, ref, axis):
    n = ref.shape[axis] // 2
    for c in (core(place), 1 - core(place)):
        part = pl.ds(pl.multiple_of(c * n, n), n)
        yield ref[part, :] if axis == 0 else ref[:, part]


def parts_kernel(place, own, other, w_in, w_out, out):
    hid = w_in.shape[1]
    (in_own, in_other), (out_own, out_other) = halves(place, w_in, 0), halves(place, w_out, 1)
    out[:, :hid] = (
        dot(own[0], in_own, ((1,), (0,))) + dot(other[0], in_other, ((1,), (0,)))
    ).astype(bf16)
    out[:, hid:] = (
        dot(own[1], out_own, ((1,), (1,))) + dot(other[1], out_other, ((1,), (1,)))
    ).astype(bf16)


def gelu_kernel(place, got, dh, act):
    hid = dh.shape[1]
    total = got[0].astype(f32)
    for q in range(1, got.shape[0]):
        total = total + got[q].astype(f32)
    gelu_value, gelu_slope = gelu_pair(total[:, :hid])
    dh[...] = (total[:, hid:] * gelu_slope).astype(bf16)
    act[...] = gelu_value.astype(bf16)


def back_kernel(place, dh, own, left, right, far, mine, theirs, w):
    y, c = place[0] >> 1, core(place)
    hs = 4
    f = own.shape[0] // (2 * hs)
    for out, at in ((theirs, 1 - c), (mine, c)):
        for src, q in ((own, y), (left, (y + 3) & 3), (right, (y + 1) & 3), (far, (y + 2) & 3)):
            for h in range(hs):
                rows = src[pl.ds(pl.multiple_of((h * 2 + at) * f, f), f), :]
                w[pl.ds(pl.multiple_of((h * 4 + q) * f, f), f), :] = rows
        out[...] = dot(dh[...], w[...], ((1,), (1,))).astype(out.dtype)


def pack_kernel(place, mine, got, out):
    ls, hs, rows, n = out.shape
    for h in range(hs):
        cols = slice(h * n, (h + 1) * n)
        both = (mine[:, cols] + got[:, cols].astype(f32)).astype(bf16)
        out[:, h] = both.reshape(ls, rows, n)


def sum_kernel(place, got, _, out):
    ls, hs, inner, n = got.shape
    total = got[:, 0].astype(f32)
    for h in range(1, hs):
        total = total + got[:, h].astype(f32)
    rows = ls * inner
    row = lax.broadcasted_iota(jnp.int32, (rows, rows), 0)
    col = lax.broadcasted_iota(jnp.int32, (rows, rows), 1)
    perm = as_bf16(col == (row // 4) % ls * inner + row // (4 * ls) * 4 + row % 4)
    out[...] = dot(perm, total.astype(bf16).reshape(rows, n), ((1,), (0,))).astype(bf16)


def token_kernel(place, eid, slot, got, out):
    quarters, f, toks = out.shape
    row = lax.broadcasted_iota(jnp.int32, (got.shape[0], toks), 0)
    take = as_bf16((row // 4 == eid[...]) & (row % 4 == slot[...]))
    picked = dot(got[...], take, ((0,), (0,))).astype(bf16)
    for q in range(quarters):
        out[q] = picked[q * f : (q + 1) * f]


def grads_kernel(place, own, other, dh, act, g_in, g_out, done):
    done[...] = jnp.zeros_like(done)
    n = own.shape[2]
    for src, c in ((own, core(place)), (other, 1 - core(place))):
        part = pl.ds(pl.multiple_of(c * n, n), n)
        g_in[part, :] = dot(src[0], dh[...], ((0,), (0,))).astype(bf16)
        g_out[:, part] = dot(act[...], src[1], ((0,), (0,))).astype(bf16)


def exchange(x, axes):
    return lax.all_to_all(x, axes, split_axis=0, concat_axis=0, tiled=True)


def other_core(x):
    return lax.ppermute(x, "c", [(0, 1), (1, 0)])


def over_y(x, step):
    return lax.ppermute(x, "y", [(y, (y + step) % 4) for y in range(4)])


def local(tokens, cotangent, gate_value, expert_id, token_slot, w_in, w_out):
    ys, xs, ls, hs = (lax.axis_size(a) for a in ("y", "x", "l", "h"))
    width, hid = w_in.shape[1:]
    toks = tokens.shape[0]
    w_in, w_out = w_in[0], w_out[0]
    eid, slot, gate = (a.reshape(1, toks) for a in (expert_id, token_slot, gate_value))
    groups = ys * xs * ls
    rows, part, f = groups * 4, width // 2, width // 8
    chunk = rows // ys
    sent, w_pass = call(
        dispatch_kernel,
        [((groups * 8, part), bf16), (w_in.shape, bf16)],
        eid,
        slot,
        gate,
        tokens,
        cotangent,
        w_in,
        scratch=[
            pltpu.VMEM((1, toks), jnp.int32),
            pltpu.VMEM((1, toks), jnp.int32),
            pltpu.VMEM((1, toks), f32),
            pltpu.VMEM((ys, toks, part), bf16),
            pltpu.VMEM((ys, toks, part), bf16),
            pltpu.SemaphoreType.DMA((4 + 2 * ys,)),
        ],
        fetch=True,
    )
    got = exchange(sent.reshape(groups, 8, part), ("y", "x", "l")).reshape(groups * 8, part)
    left, right = over_y(w_pass, 1), over_y(w_pass, -1)
    far = over_y(right, -1)
    arrived = tuple(a[:16, :128] for a in (left, right))
    (own,) = call(regroup_kernel, [((2, rows, part), bf16)], got, after=arrived)
    other = other_core(own)
    (parts,) = call(parts_kernel, [((rows, 2 * hid), bf16)], own, other, w_in, w_out)
    got = exchange(parts.reshape(ys, chunk, 2 * hid), "y")
    dh, act = call(gelu_kernel, [((chunk, hid), bf16)] * 2, got)
    mine, theirs = call(
        back_kernel,
        [((chunk, ys * part), f32), ((chunk, ys * part), bf16)],
        dh,
        w_in,
        left,
        right,
        far,
        scratch=[pltpu.VMEM((ys * part, hid), bf16)],
    )
    got = other_core(theirs)
    (sent,) = call(pack_kernel, [((ls, hs, xs * 4, part), bf16)], mine, got)
    got = exchange(sent.reshape(ls * hs, xs * 4, part), ("l", "h"))
    dh, act = (lax.all_gather(a, "y", axis=0, tiled=True) for a in (dh, act))
    g_in, g_out, done = call(
        grads_kernel,
        [((width, hid), bf16), ((hid, width), bf16), ((8, 128), f32)],
        own,
        other,
        dh,
        act,
    )
    (sent,) = call(
        sum_kernel, [((chunk, part), bf16)], got.reshape(ls, hs, xs * 4, part), after=(done,)
    )
    got = exchange(sent.reshape(xs, ls * 4, part), "x").reshape(chunk, part)
    (grad_t,) = call(token_kernel, [((ys, f, toks), bf16)], eid, slot, got)
    return jnp.transpose(grad_t, (2, 0, 1)), g_in[None], g_out[None]


def solution(mesh):
    dp, expert, mp = mesh.devices.shape
    fine = Mesh(mesh.devices.reshape(dp, 4, expert // 4, mp // 2, 2), ("y", "x", "l", "h", "c"))
    group, ffn = ("y", "x", "l"), ("h", "c")
    in_specs = (
        P(group, None),
        P(group, None),
        P(group),
        P(group),
        P(group),
        P(("x", "l"), "y", ffn),
        P(("x", "l"), ffn, "y"),
    )
    out_specs = (P(group, None, ffn), P(("x", "l"), "y", ffn), P(("x", "l"), ffn, "y"))
    return jax.shard_map(local, mesh=fine, in_specs=in_specs, out_specs=out_specs, check_vma=False)
```

```python
import jax
import jax.numpy as jnp
from jax import lax
from jax.experimental import pallas as pl
from jax.experimental.pallas import tpu as pltpu
from jax.sharding import Mesh, PartitionSpec as P

tanh_scale = 0.7978845608028654
cubic_coef = 0.044715
f32 = jnp.float32
bf16 = jnp.bfloat16


def gelu_pair(pre_act):
    tanh_arg = tanh_scale * (pre_act + cubic_coef * pre_act * pre_act * pre_act)
    tanh_val = jnp.tanh(tanh_arg)
    gelu_value = 0.5 * pre_act * (1.0 + tanh_val)
    gelu_slope = 0.5 * (1.0 + tanh_val) + 0.5 * pre_act * (
        1.0 - tanh_val * tanh_val
    ) * tanh_scale * (1.0 + 3.0 * cubic_coef * pre_act * pre_act)
    return (gelu_value, gelu_slope)


def dot(a, b, dims):
    return lax.dot_general(a, b, ((dims[0], dims[1]), ((), ())), preferred_element_type=f32)


def size(shape):
    n = 1
    for s in shape:
        n *= s
    return n


def call(kernel, outs, *args, scratch=(), fetch=False, after=()):
    moved = sum(a.size * a.dtype.itemsize for a in args) + sum(
        jnp.dtype(d).itemsize * size(s) for s, d in outs
    )
    place = (lax.axis_index("y") * 2 + lax.axis_index("c")).astype(jnp.int32).reshape(1)
    space = pltpu.HBM if fetch else pltpu.VMEM
    return pl.pallas_call(
        kernel,
        out_shape=[jax.ShapeDtypeStruct(s, d) for s, d in outs],
        in_specs=[pl.BlockSpec(memory_space=pltpu.SMEM)]
        + [pl.BlockSpec(memory_space=space)] * len(args)
        + [pl.BlockSpec(memory_space=pl.ANY)] * len(after),
        out_specs=[pl.BlockSpec(memory_space=pltpu.VMEM)] * len(outs),
        scratch_shapes=scratch,
        compiler_params=pltpu.CompilerParams(vmem_limit_bytes=(60 if fetch else 16) * 1024 * 1024),
        cost_estimate=pl.CostEstimate(flops=0, bytes_accessed=moved, transcendentals=0),
    )(place, *args, *after)


def core(place):
    return place[0] & 1


def as_bf16(mask):
    return mask.astype(f32).astype(bf16)


def dispatch_kernel(
    place, eid, slot, gate, tok, cot, w_in, out, w_pass, eid_v, slot_v, gate_v, tok_v, cot_v, sems
):
    quarters, toks, feats = tok_v.shape
    count = out.shape[0] // quarters
    copies = [
        pltpu.make_async_copy(src, dst, sems.at[i])
        for i, (src, dst) in enumerate(((eid, eid_v), (slot, slot_v), (gate, gate_v)))
    ]
    for src, dst in ((tok, tok_v), (cot, cot_v)):
        for q in range(quarters):
            cols = pl.ds(pl.multiple_of((2 * q + core(place)) * feats, feats), feats)
            copies.append(pltpu.make_async_copy(src.at[:, cols], dst.at[q], sems.at[len(copies)]))
    copies.append(pltpu.make_async_copy(w_in, w_pass, sems.at[len(copies)]))
    for copy in copies:
        copy.start()
    for copy in copies[:3]:
        copy.wait()
    row = lax.broadcasted_iota(jnp.int32, (count, toks), 0)
    hit = (row // 8 == eid_v[...]) & (row % 4 == slot_v[...])
    is_x = row % 8 < 4
    take_x = as_bf16(hit & is_x)
    take_dy = as_bf16(hit & ~is_x)
    row_gate = jnp.sum(jnp.where(hit, gate_v[...], 0.0), axis=1, keepdims=True)
    for copy in copies[3:-1]:
        copy.wait()
    for q in range(quarters):
        got_x = dot(take_x, tok_v[q], ((1,), (0,)))
        got_dy = row_gate * dot(take_dy, cot_v[q], ((1,), (0,)))
        out[q * count : (q + 1) * count] = (got_x + got_dy).astype(bf16)
    copies[-1].wait()


def regroup_kernel(place, got, _, __, out):
    rows, xs = out.shape[1] // 4, 4
    count = 2 * rows
    n = lax.broadcasted_iota(jnp.int32, (count, count), 0)
    col = lax.broadcasted_iota(jnp.int32, (count, count), 1)
    which, at_l, x, slot = n // rows, (n % rows) // (4 * xs), (n // 4) % xs, n % 4
    perm = as_bf16(col == ((x * (rows // (4 * xs)) + at_l) * 2 + which) * 4 + slot)
    for y in range(4):
        moved = dot(perm, got[y * count : (y + 1) * count], ((1,), (0,))).astype(bf16)
        out[0, y * rows : (y + 1) * rows] = moved[:rows]
        out[1, y * rows : (y + 1) * rows] = moved[rows:]


def halves(place, ref, axis):
    n = ref.shape[axis] // 2
    for c in (core(place), 1 - core(place)):
        part = pl.ds(pl.multiple_of(c * n, n), n)
        yield ref[part, :] if axis == 0 else ref[:, part]


def parts_kernel(place, own, other, w_in, w_out, _, out):
    hid = w_in.shape[1]
    (in_own, in_other), (out_own, out_other) = halves(place, w_in, 0), halves(place, w_out, 1)
    out[:, :hid] = (
        dot(own[0], in_own, ((1,), (0,))) + dot(other[0], in_other, ((1,), (0,)))
    ).astype(bf16)
    out[:, hid:] = (
        dot(own[1], out_own, ((1,), (1,))) + dot(other[1], out_other, ((1,), (1,)))
    ).astype(bf16)


def gelu_kernel(place, got, dh, act):
    hid = dh.shape[1]
    total = got[0].astype(f32)
    for q in range(1, got.shape[0]):
        total = total + got[q].astype(f32)
    gelu_value, gelu_slope = gelu_pair(total[:, :hid])
    dh[...] = (total[:, hid:] * gelu_slope).astype(bf16)
    act[...] = gelu_value.astype(bf16)


def back_kernel(place, dh, own, left, right, far, mine, theirs, w):
    y, c = place[0] >> 1, core(place)
    hs = 4
    f = own.shape[0] // (2 * hs)
    for out, at in ((theirs, 1 - c), (mine, c)):
        for src, q in ((own, y), (left, (y + 3) & 3), (right, (y + 1) & 3), (far, (y + 2) & 3)):
            for h in range(hs):
                rows = src[pl.ds(pl.multiple_of((h * 2 + at) * f, f), f), :]
                w[pl.ds(pl.multiple_of((h * 4 + q) * f, f), f), :] = rows
        out[...] = dot(dh[...], w[...], ((1,), (1,))).astype(out.dtype)


def pack_kernel(place, mine, got, out):
    ls, hs, rows, n = out.shape
    for h in range(hs):
        cols = slice(h * n, (h + 1) * n)
        both = (mine[:, cols] + got[:, cols].astype(f32)).astype(bf16)
        out[:, h] = both.reshape(ls, rows, n)


def sum_kernel(place, got, _, out):
    ls, hs, inner, n = got.shape
    total = got[:, 0].astype(f32)
    for h in range(1, hs):
        total = total + got[:, h].astype(f32)
    rows = ls * inner
    row = lax.broadcasted_iota(jnp.int32, (rows, rows), 0)
    col = lax.broadcasted_iota(jnp.int32, (rows, rows), 1)
    perm = as_bf16(col == (row // 4) % ls * inner + row // (4 * ls) * 4 + row % 4)
    out[...] = dot(perm, total.astype(bf16).reshape(rows, n), ((1,), (0,))).astype(bf16)


def token_kernel(place, eid, slot, got, out):
    quarters, f, toks = out.shape
    row = lax.broadcasted_iota(jnp.int32, (got.shape[0], toks), 0)
    take = as_bf16((row // 4 == eid[...]) & (row % 4 == slot[...]))
    picked = dot(got[...], take, ((0,), (0,))).astype(bf16)
    for q in range(quarters):
        out[q] = picked[q * f : (q + 1) * f]


def grads_kernel(place, own, other, dh, act, g_in, g_out, done):
    done[...] = jnp.zeros_like(done)
    n = own.shape[2]
    for src, c in ((own, core(place)), (other, 1 - core(place))):
        part = pl.ds(pl.multiple_of(c * n, n), n)
        g_in[part, :] = dot(src[0], dh[...], ((0,), (0,))).astype(bf16)
        g_out[:, part] = dot(act[...], src[1], ((0,), (0,))).astype(bf16)


def exchange(x, axes):
    return lax.all_to_all(x, axes, split_axis=0, concat_axis=0, tiled=True)


def other_core(x):
    return lax.ppermute(x, "c", [(0, 1), (1, 0)])


def over_y(x, step):
    return lax.ppermute(x, "y", [(y, (y + step) % 4) for y in range(4)])


def local(tokens, cotangent, gate_value, expert_id, token_slot, w_in, w_out):
    ys, xs, ls, hs = (lax.axis_size(a) for a in ("y", "x", "l", "h"))
    width, hid = w_in.shape[1:]
    toks = tokens.shape[0]
    w_in, w_out = w_in[0], w_out[0]
    eid, slot, gate = (a.reshape(1, toks) for a in (expert_id, token_slot, gate_value))
    groups = ys * xs * ls
    rows, part, f = groups * 4, width // 2, width // 8
    chunk = rows // ys
    sent, w_pass = call(
        dispatch_kernel,
        [((groups * 8, part), bf16), (w_in.shape, bf16)],
        eid,
        slot,
        gate,
        tokens,
        cotangent,
        w_in,
        scratch=[
            pltpu.VMEM((1, toks), jnp.int32),
            pltpu.VMEM((1, toks), jnp.int32),
            pltpu.VMEM((1, toks), f32),
            pltpu.VMEM((ys, toks, part), bf16),
            pltpu.VMEM((ys, toks, part), bf16),
            pltpu.SemaphoreType.DMA((4 + 2 * ys,)),
        ],
        fetch=True,
    )
    got = exchange(sent.reshape(groups, 8, part), ("y", "x", "l")).reshape(groups * 8, part)
    left, right = over_y(w_pass, 1), over_y(w_pass, -1)
    far = over_y(right, -1)
    arrived = tuple(a[:16, :128] for a in (left, right))
    (own,) = call(regroup_kernel, [((2, rows, part), bf16)], got, after=arrived)
    other = other_core(own)
    (parts,) = call(
        parts_kernel, [((rows, 2 * hid), bf16)], own, other, w_in, w_out, after=(far[:16, :128],)
    )
    got = exchange(parts.reshape(ys, chunk, 2 * hid), "y")
    dh, act = call(gelu_kernel, [((chunk, hid), bf16)] * 2, got)
    mine, theirs = call(
        back_kernel,
        [((chunk, ys * part), f32), ((chunk, ys * part), bf16)],
        dh,
        w_in,
        left,
        right,
        far,
        scratch=[pltpu.VMEM((ys * part, hid), bf16)],
    )
    got = other_core(theirs)
    (sent,) = call(pack_kernel, [((ls, hs, xs * 4, part), bf16)], mine, got)
    got = exchange(sent.reshape(ls * hs, xs * 4, part), ("l", "h"))
    dh, act = (lax.all_gather(a, "y", axis=0, tiled=True) for a in (dh, act))
    g_in, g_out, done = call(
        grads_kernel,
        [((width, hid), bf16), ((hid, width), bf16), ((8, 128), f32)],
        own,
        other,
        dh,
        act,
    )
    (sent,) = call(
        sum_kernel, [((chunk, part), bf16)], got.reshape(ls, hs, xs * 4, part), after=(done,)
    )
    got = exchange(sent.reshape(xs, ls * 4, part), "x").reshape(chunk, part)
    (grad_t,) = call(token_kernel, [((ys, f, toks), bf16)], eid, slot, got)
    return jnp.transpose(grad_t, (2, 0, 1)), g_in[None], g_out[None]


def solution(mesh):
    dp, expert, mp = mesh.devices.shape
    fine = Mesh(mesh.devices.reshape(dp, 4, expert // 4, mp // 2, 2), ("y", "x", "l", "h", "c"))
    group, ffn = ("y", "x", "l"), ("h", "c")
    in_specs = (
        P(group, None),
        P(group, None),
        P(group),
        P(group),
        P(group),
        P(("x", "l"), "y", ffn),
        P(("x", "l"), ffn, "y"),
    )
    out_specs = (P(group, None, ffn), P(("x", "l"), "y", ffn), P(("x", "l"), ffn, "y"))
    return jax.shard_map(local, mesh=fine, in_specs=in_specs, out_specs=out_specs, check_vma=False)
```

```python
import jax
import jax.numpy as jnp
from jax import lax
from jax.experimental import pallas as pl
from jax.experimental.pallas import tpu as pltpu
from jax.sharding import Mesh, PartitionSpec as P

tanh_scale = 0.7978845608028654
cubic_coef = 0.044715
f32 = jnp.float32
bf16 = jnp.bfloat16


def gelu_pair(pre_act):
    tanh_arg = tanh_scale * (pre_act + cubic_coef * pre_act * pre_act * pre_act)
    tanh_val = jnp.tanh(tanh_arg)
    gelu_value = 0.5 * pre_act * (1.0 + tanh_val)
    gelu_slope = 0.5 * (1.0 + tanh_val) + 0.5 * pre_act * (
        1.0 - tanh_val * tanh_val
    ) * tanh_scale * (1.0 + 3.0 * cubic_coef * pre_act * pre_act)
    return (gelu_value, gelu_slope)


def dot(a, b, dims):
    return lax.dot_general(a, b, ((dims[0], dims[1]), ((), ())), preferred_element_type=f32)


def size(shape):
    n = 1
    for s in shape:
        n *= s
    return n


def call(kernel, outs, *args, scratch=(), fetch=False, after=()):
    moved = sum(a.size * a.dtype.itemsize for a in args) + sum(
        jnp.dtype(d).itemsize * size(s) for s, d in outs
    )
    place = (lax.axis_index("y") * 2 + lax.axis_index("c")).astype(jnp.int32).reshape(1)
    space = pltpu.HBM if fetch else pltpu.VMEM
    return pl.pallas_call(
        kernel,
        out_shape=[jax.ShapeDtypeStruct(s, d) for s, d in outs],
        in_specs=[pl.BlockSpec(memory_space=pltpu.SMEM)]
        + [pl.BlockSpec(memory_space=space)] * len(args)
        + [pl.BlockSpec(memory_space=pl.ANY)] * len(after),
        out_specs=[pl.BlockSpec(memory_space=pltpu.VMEM)] * len(outs),
        scratch_shapes=scratch,
        compiler_params=pltpu.CompilerParams(vmem_limit_bytes=(60 if fetch else 16) * 1024 * 1024),
        cost_estimate=pl.CostEstimate(flops=0, bytes_accessed=moved, transcendentals=0),
    )(place, *args, *after)


def core(place):
    return place[0] & 1


def as_bf16(mask):
    return mask.astype(f32).astype(bf16)


def dispatch_kernel(
    place, eid, slot, gate, tok, cot, w_in, out, w_pass, eid_v, slot_v, gate_v, tok_v, cot_v, sems
):
    quarters, toks, feats = tok_v.shape
    count = out.shape[0] // quarters
    copies = [
        pltpu.make_async_copy(src, dst, sems.at[i])
        for i, (src, dst) in enumerate(((eid, eid_v), (slot, slot_v), (gate, gate_v)))
    ]
    for src, dst in ((tok, tok_v), (cot, cot_v)):
        for q in range(quarters):
            cols = pl.ds(pl.multiple_of((2 * q + core(place)) * feats, feats), feats)
            copies.append(pltpu.make_async_copy(src.at[:, cols], dst.at[q], sems.at[len(copies)]))
    copies.append(pltpu.make_async_copy(w_in, w_pass, sems.at[len(copies)]))
    for copy in copies:
        copy.start()
    for copy in copies[:3]:
        copy.wait()
    row = lax.broadcasted_iota(jnp.int32, (count, toks), 0)
    hit = (row // 8 == eid_v[...]) & (row % 4 == slot_v[...])
    is_x = row % 8 < 4
    take_x = as_bf16(hit & is_x)
    take_dy = as_bf16(hit & ~is_x)
    row_gate = jnp.sum(jnp.where(hit, gate_v[...], 0.0), axis=1, keepdims=True)
    for copy in copies[3:-1]:
        copy.wait()
    for q in range(quarters):
        got_x = dot(take_x, tok_v[q], ((1,), (0,)))
        got_dy = row_gate * dot(take_dy, cot_v[q], ((1,), (0,)))
        out[q * count : (q + 1) * count] = (got_x + got_dy).astype(bf16)
    copies[-1].wait()


def regroup_kernel(place, got, _, __, out):
    rows, xs = out.shape[1] // 4, 4
    count = 2 * rows
    n = lax.broadcasted_iota(jnp.int32, (count, count), 0)
    col = lax.broadcasted_iota(jnp.int32, (count, count), 1)
    which, at_l, x, slot = n // rows, (n % rows) // (4 * xs), (n // 4) % xs, n % 4
    perm = as_bf16(col == ((x * (rows // (4 * xs)) + at_l) * 2 + which) * 4 + slot)
    for y in range(4):
        moved = dot(perm, got[y * count : (y + 1) * count], ((1,), (0,))).astype(bf16)
        out[0, y * rows : (y + 1) * rows] = moved[:rows]
        out[1, y * rows : (y + 1) * rows] = moved[rows:]


def halves(place, ref, axis):
    n = ref.shape[axis] // 2
    for c in (core(place), 1 - core(place)):
        part = pl.ds(pl.multiple_of(c * n, n), n)
        yield ref[part, :] if axis == 0 else ref[:, part]


def parts_kernel(place, own, other, w_in, w_out, out):
    hid = w_in.shape[1]
    (in_own, in_other), (out_own, out_other) = halves(place, w_in, 0), halves(place, w_out, 1)
    out[:, :hid] = (
        dot(own[0], in_own, ((1,), (0,))) + dot(other[0], in_other, ((1,), (0,)))
    ).astype(bf16)
    out[:, hid:] = (
        dot(own[1], out_own, ((1,), (1,))) + dot(other[1], out_other, ((1,), (1,)))
    ).astype(bf16)


def gelu_kernel(place, got, dh, act):
    hid = dh.shape[1]
    total = got[0].astype(f32)
    for q in range(1, got.shape[0]):
        total = total + got[q].astype(f32)
    gelu_value, gelu_slope = gelu_pair(total[:, :hid])
    dh[...] = (total[:, hid:] * gelu_slope).astype(bf16)
    act[...] = gelu_value.astype(bf16)


def back_kernel(place, dh, own, left, right, far, mine, theirs, w):
    y, c = place[0] >> 1, core(place)
    hs = 4
    f = own.shape[0] // (2 * hs)
    for out, at in ((theirs, 1 - c), (mine, c)):
        for src, q in ((own, y), (left, (y + 3) & 3), (right, (y + 1) & 3), (far, (y + 2) & 3)):
            for h in range(hs):
                rows = src[pl.ds(pl.multiple_of((h * 2 + at) * f, f), f), :]
                w[pl.ds(pl.multiple_of((h * 4 + q) * f, f), f), :] = rows
        out[...] = dot(dh[...], w[...], ((1,), (1,))).astype(out.dtype)


def pack_kernel(place, mine, got, out):
    ls, hs, rows, n = out.shape
    for h in range(hs):
        cols = slice(h * n, (h + 1) * n)
        both = (mine[:, cols] + got[:, cols].astype(f32)).astype(bf16)
        out[:, h] = both.reshape(ls, rows, n)


def sum_kernel(place, got, _, out):
    ls, hs, inner, n = got.shape
    total = got[:, 0].astype(f32)
    for h in range(1, hs):
        total = total + got[:, h].astype(f32)
    rows = ls * inner
    row = lax.broadcasted_iota(jnp.int32, (rows, rows), 0)
    col = lax.broadcasted_iota(jnp.int32, (rows, rows), 1)
    perm = as_bf16(col == (row // 4) % ls * inner + row // (4 * ls) * 4 + row % 4)
    out[...] = dot(perm, total.astype(bf16).reshape(rows, n), ((1,), (0,))).astype(bf16)


def token_kernel(place, eid, slot, got, out):
    quarters, f, toks = out.shape
    row = lax.broadcasted_iota(jnp.int32, (got.shape[0], toks), 0)
    take = as_bf16((row // 4 == eid[...]) & (row % 4 == slot[...]))
    picked = dot(got[...], take, ((0,), (0,))).astype(bf16)
    for q in range(quarters):
        out[q] = picked[q * f : (q + 1) * f]


def grads_kernel(place, own, other, dh, act, g_in, g_out, done):
    done[...] = jnp.zeros_like(done)
    n = own.shape[2]
    for src, c in ((own, core(place)), (other, 1 - core(place))):
        part = pl.ds(pl.multiple_of(c * n, n), n)
        g_in[part, :] = dot(src[0], dh[...], ((0,), (0,))).astype(bf16)
        g_out[:, part] = dot(act[...], src[1], ((0,), (0,))).astype(bf16)


def exchange(x, axes):
    return lax.all_to_all(x, axes, split_axis=0, concat_axis=0, tiled=True)


def other_core(x):
    return lax.ppermute(x, "c", [(0, 1), (1, 0)])


def over_y(x, step):
    return lax.ppermute(x, "y", [(y, (y + step) % 4) for y in range(4)])


def local(tokens, cotangent, gate_value, expert_id, token_slot, w_in, w_out):
    ys, xs, ls, hs = (lax.axis_size(a) for a in ("y", "x", "l", "h"))
    width, hid = w_in.shape[1:]
    toks = tokens.shape[0]
    w_in, w_out = w_in[0], w_out[0]
    eid, slot, gate = (a.reshape(1, toks) for a in (expert_id, token_slot, gate_value))
    groups = ys * xs * ls
    rows, part, f = groups * 4, width // 2, width // 8
    chunk = rows // ys
    sent, w_pass = call(
        dispatch_kernel,
        [((groups * 8, part), bf16), (w_in.shape, bf16)],
        eid,
        slot,
        gate,
        tokens,
        cotangent,
        w_in,
        scratch=[
            pltpu.VMEM((1, toks), jnp.int32),
            pltpu.VMEM((1, toks), jnp.int32),
            pltpu.VMEM((1, toks), f32),
            pltpu.VMEM((ys, toks, part), bf16),
            pltpu.VMEM((ys, toks, part), bf16),
            pltpu.SemaphoreType.DMA((4 + 2 * ys,)),
        ],
        fetch=True,
    )
    got = exchange(sent.reshape(groups, 8, part), ("y", "x", "l")).reshape(groups * 8, part)
    left, right = over_y(w_pass, 1), over_y(w_pass, -1)
    far = over_y(left, 1)
    arrived = tuple(a[:16, :128] for a in (left, right))
    (own,) = call(regroup_kernel, [((2, rows, part), bf16)], got, after=arrived)
    other = other_core(own)
    (parts,) = call(parts_kernel, [((rows, 2 * hid), bf16)], own, other, w_in, w_out)
    got = exchange(parts.reshape(ys, chunk, 2 * hid), "y")
    dh, act = call(gelu_kernel, [((chunk, hid), bf16)] * 2, got)
    mine, theirs = call(
        back_kernel,
        [((chunk, ys * part), f32), ((chunk, ys * part), bf16)],
        dh,
        w_in,
        left,
        right,
        far,
        scratch=[pltpu.VMEM((ys * part, hid), bf16)],
    )
    got = other_core(theirs)
    (sent,) = call(pack_kernel, [((ls, hs, xs * 4, part), bf16)], mine, got)
    got = exchange(sent.reshape(ls * hs, xs * 4, part), ("l", "h"))
    dh, act = (lax.all_gather(a, "y", axis=0, tiled=True) for a in (dh, act))
    g_in, g_out, done = call(
        grads_kernel,
        [((width, hid), bf16), ((hid, width), bf16), ((8, 128), f32)],
        own,
        other,
        dh,
        act,
    )
    (sent,) = call(
        sum_kernel, [((chunk, part), bf16)], got.reshape(ls, hs, xs * 4, part), after=(done,)
    )
    got = exchange(sent.reshape(xs, ls * 4, part), "x").reshape(chunk, part)
    (grad_t,) = call(token_kernel, [((ys, f, toks), bf16)], eid, slot, got)
    return jnp.transpose(grad_t, (2, 0, 1)), g_in[None], g_out[None]


def solution(mesh):
    dp, expert, mp = mesh.devices.shape
    fine = Mesh(mesh.devices.reshape(dp, 4, expert // 4, mp // 2, 2), ("y", "x", "l", "h", "c"))
    group, ffn = ("y", "x", "l"), ("h", "c")
    in_specs = (
        P(group, None),
        P(group, None),
        P(group),
        P(group),
        P(group),
        P(("x", "l"), "y", ffn),
        P(("x", "l"), ffn, "y"),
    )
    out_specs = (P(group, None, ffn), P(("x", "l"), "y", ffn), P(("x", "l"), ffn, "y"))
    return jax.shard_map(local, mesh=fine, in_specs=in_specs, out_specs=out_specs, check_vma=False)
```

```python
import jax
import jax.numpy as jnp
from jax import lax
from jax.experimental import pallas as pl
from jax.experimental.pallas import tpu as pltpu
from jax.sharding import Mesh, PartitionSpec as P

tanh_scale = 0.7978845608028654
cubic_coef = 0.044715
f32 = jnp.float32
bf16 = jnp.bfloat16


def gelu_pair(pre_act):
    tanh_arg = tanh_scale * (pre_act + cubic_coef * pre_act * pre_act * pre_act)
    tanh_val = jnp.tanh(tanh_arg)
    gelu_value = 0.5 * pre_act * (1.0 + tanh_val)
    gelu_slope = 0.5 * (1.0 + tanh_val) + 0.5 * pre_act * (
        1.0 - tanh_val * tanh_val
    ) * tanh_scale * (1.0 + 3.0 * cubic_coef * pre_act * pre_act)
    return (gelu_value, gelu_slope)


def dot(a, b, dims):
    return lax.dot_general(a, b, ((dims[0], dims[1]), ((), ())), preferred_element_type=f32)


def size(shape):
    n = 1
    for s in shape:
        n *= s
    return n


def call(kernel, outs, *args, scratch=(), fetch=False, after=()):
    moved = sum(a.size * a.dtype.itemsize for a in args) + sum(
        jnp.dtype(d).itemsize * size(s) for s, d in outs
    )
    place = (lax.axis_index("y") * 2 + lax.axis_index("c")).astype(jnp.int32).reshape(1)
    space = pltpu.HBM if fetch else pltpu.VMEM
    return pl.pallas_call(
        kernel,
        out_shape=[jax.ShapeDtypeStruct(s, d) for s, d in outs],
        in_specs=[pl.BlockSpec(memory_space=pltpu.SMEM)]
        + [pl.BlockSpec(memory_space=space)] * len(args)
        + [pl.BlockSpec(memory_space=pl.ANY)] * len(after),
        out_specs=[pl.BlockSpec(memory_space=pltpu.VMEM)] * len(outs),
        scratch_shapes=scratch,
        compiler_params=pltpu.CompilerParams(vmem_limit_bytes=(60 if fetch else 16) * 1024 * 1024),
        cost_estimate=pl.CostEstimate(flops=0, bytes_accessed=moved, transcendentals=0),
    )(place, *args, *after)


def core(place):
    return place[0] & 1


def as_bf16(mask):
    return mask.astype(f32).astype(bf16)


def dispatch_kernel(
    place, eid, slot, gate, tok, cot, w_in, out, w_pass, eid_v, slot_v, gate_v, tok_v, cot_v, sems
):
    quarters, toks, feats = tok_v.shape
    count = out.shape[0] // quarters
    copies = [
        pltpu.make_async_copy(src, dst, sems.at[i])
        for i, (src, dst) in enumerate(((eid, eid_v), (slot, slot_v), (gate, gate_v)))
    ]
    for src, dst in ((tok, tok_v), (cot, cot_v)):
        for q in range(quarters):
            cols = pl.ds(pl.multiple_of((2 * q + core(place)) * feats, feats), feats)
            copies.append(pltpu.make_async_copy(src.at[:, cols], dst.at[q], sems.at[len(copies)]))
    copies.append(pltpu.make_async_copy(w_in, w_pass, sems.at[len(copies)]))
    for copy in copies:
        copy.start()
    for copy in copies[:3]:
        copy.wait()
    row = lax.broadcasted_iota(jnp.int32, (count, toks), 0)
    hit = (row // 8 == eid_v[...]) & (row % 4 == slot_v[...])
    is_x = row % 8 < 4
    take_x = as_bf16(hit & is_x)
    take_dy = as_bf16(hit & ~is_x)
    row_gate = jnp.sum(jnp.where(hit, gate_v[...], 0.0), axis=1, keepdims=True)
    for copy in copies[3:-1]:
        copy.wait()
    for q in range(quarters):
        got_x = dot(take_x, tok_v[q], ((1,), (0,)))
        got_dy = row_gate * dot(take_dy, cot_v[q], ((1,), (0,)))
        out[q * count : (q + 1) * count] = (got_x + got_dy).astype(bf16)
    copies[-1].wait()


def regroup_kernel(place, got, _, __, ___, out):
    rows, xs = out.shape[1] // 4, 4
    count = 2 * rows
    n = lax.broadcasted_iota(jnp.int32, (count, count), 0)
    col = lax.broadcasted_iota(jnp.int32, (count, count), 1)
    which, at_l, x, slot = n // rows, (n % rows) // (4 * xs), (n // 4) % xs, n % 4
    perm = as_bf16(col == ((x * (rows // (4 * xs)) + at_l) * 2 + which) * 4 + slot)
    for y in range(4):
        moved = dot(perm, got[y * count : (y + 1) * count], ((1,), (0,))).astype(bf16)
        out[0, y * rows : (y + 1) * rows] = moved[:rows]
        out[1, y * rows : (y + 1) * rows] = moved[rows:]


def halves(place, ref, axis):
    n = ref.shape[axis] // 2
    for c in (core(place), 1 - core(place)):
        part = pl.ds(pl.multiple_of(c * n, n), n)
        yield ref[part, :] if axis == 0 else ref[:, part]


def parts_kernel(place, own, other, w_in, w_out, _, out):
    hid = w_in.shape[1]
    in_own, in_other = halves(place, w_in, 0)
    out[:, :hid] = (
        dot(own[0], in_own, ((1,), (0,))) + dot(other[0], in_other, ((1,), (0,)))
    ).astype(bf16)
    out_own, out_other = halves(place, w_out, 1)
    out[:, hid:] = (
        dot(own[1], out_own, ((1,), (1,))) + dot(other[1], out_other, ((1,), (1,)))
    ).astype(bf16)


def back_kernel(place, got, own, left, right, far, mine, theirs, dh, act, w):
    hid = dh.shape[1]
    total = got[0].astype(f32)
    for q in range(1, got.shape[0]):
        total = total + got[q].astype(f32)
    gelu_value, gelu_slope = gelu_pair(total[:, :hid])
    dh[...] = (total[:, hid:] * gelu_slope).astype(bf16)
    act[...] = gelu_value.astype(bf16)
    y, c = place[0] >> 1, core(place)
    hs = 4
    f = own.shape[0] // (2 * hs)
    for out, at in ((theirs, 1 - c), (mine, c)):
        for src, q in ((own, y), (left, (y + 3) & 3), (right, (y + 1) & 3), (far, (y + 2) & 3)):
            for h in range(hs):
                rows = src[pl.ds(pl.multiple_of((h * 2 + at) * f, f), f), :]
                w[pl.ds(pl.multiple_of((h * 4 + q) * f, f), f), :] = rows
        out[...] = dot(dh[...], w[...], ((1,), (1,))).astype(out.dtype)


def pack_kernel(place, mine, got, out):
    ls, hs, rows, n = out.shape
    for h in range(hs):
        cols = slice(h * n, (h + 1) * n)
        both = (mine[:, cols] + got[:, cols].astype(f32)).astype(bf16)
        out[:, h] = both.reshape(ls, rows, n)


def sum_kernel(place, got, _, out):
    ls, hs, inner, n = got.shape
    total = got[:, 0].astype(f32)
    for h in range(1, hs):
        total = total + got[:, h].astype(f32)
    rows = ls * inner
    row = lax.broadcasted_iota(jnp.int32, (rows, rows), 0)
    col = lax.broadcasted_iota(jnp.int32, (rows, rows), 1)
    perm = as_bf16(col == (row // 4) % ls * inner + row // (4 * ls) * 4 + row % 4)
    out[...] = dot(perm, total.astype(bf16).reshape(rows, n), ((1,), (0,))).astype(bf16)


def token_kernel(place, eid, slot, got, out):
    quarters, f, toks = out.shape
    row = lax.broadcasted_iota(jnp.int32, (got.shape[0], toks), 0)
    take = as_bf16((row // 4 == eid[...]) & (row % 4 == slot[...]))
    picked = dot(got[...], take, ((0,), (0,))).astype(bf16)
    for q in range(quarters):
        out[q] = picked[q * f : (q + 1) * f]


def grads_kernel(place, own, other, dh, act, g_in, g_out, done):
    done[...] = jnp.zeros_like(done)
    n = own.shape[2]
    for src, c in ((own, core(place)), (other, 1 - core(place))):
        part = pl.ds(pl.multiple_of(c * n, n), n)
        g_in[part, :] = dot(src[0], dh[...], ((0,), (0,))).astype(bf16)
        g_out[:, part] = dot(act[...], src[1], ((0,), (0,))).astype(bf16)


def exchange(x, axes):
    return lax.all_to_all(x, axes, split_axis=0, concat_axis=0, tiled=True)


def other_core(x):
    return lax.ppermute(x, "c", [(0, 1), (1, 0)])


def over_y(x, step):
    return lax.ppermute(x, "y", [(y, (y + step) % 4) for y in range(4)])


def local(tokens, cotangent, gate_value, expert_id, token_slot, w_in, w_out):
    ys, xs, ls, hs = (lax.axis_size(a) for a in ("y", "x", "l", "h"))
    width, hid = w_in.shape[1:]
    toks = tokens.shape[0]
    w_in, w_out = w_in[0], w_out[0]
    eid, slot, gate = (a.reshape(1, toks) for a in (expert_id, token_slot, gate_value))
    groups = ys * xs * ls
    rows, part, f = groups * 4, width // 2, width // 8
    chunk = rows // ys
    sent, w_pass = call(
        dispatch_kernel,
        [((groups * 8, part), bf16), (w_in.shape, bf16)],
        eid,
        slot,
        gate,
        tokens,
        cotangent,
        w_in,
        scratch=[
            pltpu.VMEM((1, toks), jnp.int32),
            pltpu.VMEM((1, toks), jnp.int32),
            pltpu.VMEM((1, toks), f32),
            pltpu.VMEM((ys, toks, part), bf16),
            pltpu.VMEM((ys, toks, part), bf16),
            pltpu.SemaphoreType.DMA((4 + 2 * ys,)),
        ],
        fetch=True,
    )
    got = exchange(sent.reshape(groups, 8, part), ("y", "x", "l")).reshape(groups * 8, part)
    left, right = over_y(w_pass, 1), over_y(w_pass, -1)
    far = over_y(right, -1)
    arrived = tuple(a[:16, :128] for a in (left, right)) + (w_out,)
    (own,) = call(regroup_kernel, [((2, rows, part), bf16)], got, after=arrived)
    other = other_core(own)
    (parts,) = call(
        parts_kernel,
        [((rows, 2 * hid), bf16)],
        own,
        other,
        w_in,
        w_out,
        after=(far,),
    )
    got = exchange(parts.reshape(ys, chunk, 2 * hid), "y")
    block = ((chunk, hid), bf16)
    mine, theirs, dh, act = call(
        back_kernel,
        [((chunk, ys * part), f32), ((chunk, ys * part), bf16), block, block],
        got,
        w_in,
        left,
        right,
        far,
        scratch=[pltpu.VMEM((ys * part, hid), bf16)],
    )
    got = other_core(theirs)
    (sent,) = call(pack_kernel, [((ls, hs, xs * 4, part), bf16)], mine, got)
    got = exchange(sent.reshape(ls * hs, xs * 4, part), ("l", "h"))
    dh, act = (lax.all_gather(a, "y", axis=0, tiled=True) for a in (dh, act))
    g_in, g_out, done = call(
        grads_kernel,
        [((width, hid), bf16), ((hid, width), bf16), ((8, 128), f32)],
        own,
        other,
        dh,
        act,
    )
    (sent,) = call(
        sum_kernel, [((chunk, part), bf16)], got.reshape(ls, hs, xs * 4, part), after=(done,)
    )
    got = exchange(sent.reshape(xs, ls * 4, part), "x").reshape(chunk, part)
    (grad_t,) = call(token_kernel, [((ys, f, toks), bf16)], eid, slot, got)
    return jnp.transpose(grad_t, (2, 0, 1)), g_in[None], g_out[None]


def solution(mesh):
    dp, expert, mp = mesh.devices.shape
    fine = Mesh(mesh.devices.reshape(dp, 4, expert // 4, mp // 2, 2), ("y", "x", "l", "h", "c"))
    group, ffn = ("y", "x", "l"), ("h", "c")
    in_specs = (
        P(group, None),
        P(group, None),
        P(group),
        P(group),
        P(group),
        P(("x", "l"), "y", ffn),
        P(("x", "l"), ffn, "y"),
    )
    out_specs = (P(group, None, ffn), P(("x", "l"), "y", ffn), P(("x", "l"), ffn, "y"))
    return jax.shard_map(local, mesh=fine, in_specs=in_specs, out_specs=out_specs, check_vma=False)
```

```python
import jax
import jax.numpy as jnp
from jax import lax
from jax.experimental import pallas as pl
from jax.experimental.pallas import tpu as pltpu
from jax.sharding import Mesh, PartitionSpec as P

tanh_scale = 0.7978845608028654
cubic_coef = 0.044715
f32 = jnp.float32
bf16 = jnp.bfloat16


def gelu_pair(pre_act):
    tanh_arg = tanh_scale * (pre_act + cubic_coef * pre_act * pre_act * pre_act)
    tanh_val = jnp.tanh(tanh_arg)
    gelu_value = 0.5 * pre_act * (1.0 + tanh_val)
    gelu_slope = 0.5 * (1.0 + tanh_val) + 0.5 * pre_act * (
        1.0 - tanh_val * tanh_val
    ) * tanh_scale * (1.0 + 3.0 * cubic_coef * pre_act * pre_act)
    return (gelu_value, gelu_slope)


def dot(a, b, dims):
    return lax.dot_general(a, b, ((dims[0], dims[1]), ((), ())), preferred_element_type=f32)


def size(shape):
    n = 1
    for s in shape:
        n *= s
    return n


def call(kernel, outs, *args, scratch=(), fetch=False, after=()):
    moved = sum(a.size * a.dtype.itemsize for a in args) + sum(
        jnp.dtype(d).itemsize * size(s) for s, d in outs
    )
    place = (lax.axis_index("y") * 2 + lax.axis_index("c")).astype(jnp.int32).reshape(1)
    space = pltpu.HBM if fetch else pltpu.VMEM
    return pl.pallas_call(
        kernel,
        out_shape=[jax.ShapeDtypeStruct(s, d) for s, d in outs],
        in_specs=[pl.BlockSpec(memory_space=pltpu.SMEM)]
        + [pl.BlockSpec(memory_space=space)] * len(args)
        + [pl.BlockSpec(memory_space=pl.ANY)] * len(after),
        out_specs=[pl.BlockSpec(memory_space=pltpu.VMEM)] * len(outs),
        scratch_shapes=scratch,
        compiler_params=pltpu.CompilerParams(vmem_limit_bytes=(60 if fetch else 16) * 1024 * 1024),
        cost_estimate=pl.CostEstimate(flops=0, bytes_accessed=moved, transcendentals=0),
    )(place, *args, *after)


def core(place):
    return place[0] & 1


def as_bf16(mask):
    return mask.astype(f32).astype(bf16)


def dispatch_kernel(
    place, eid, slot, gate, tok, cot, w_in, out, w_low, w_high, eid_v, slot_v, gate_v, tok_v, cot_v, sems
):
    quarters, toks, feats = tok_v.shape
    count = out.shape[0] // quarters
    copies = [
        pltpu.make_async_copy(src, dst, sems.at[i])
        for i, (src, dst) in enumerate(((eid, eid_v), (slot, slot_v), (gate, gate_v)))
    ]
    for src, dst in ((tok, tok_v), (cot, cot_v)):
        for q in range(quarters):
            cols = pl.ds(pl.multiple_of((2 * q + core(place)) * feats, feats), feats)
            copies.append(pltpu.make_async_copy(src.at[:, cols], dst.at[q], sems.at[len(copies)]))
    half = w_in.shape[0] // 2
    for i, dst in enumerate((w_low, w_high)):
        src = w_in.at[i * half : (i + 1) * half]
        copies.append(pltpu.make_async_copy(src, dst, sems.at[len(copies)]))
    for copy in copies:
        copy.start()
    for copy in copies[:3]:
        copy.wait()
    row = lax.broadcasted_iota(jnp.int32, (count, toks), 0)
    hit = (row // 8 == eid_v[...]) & (row % 4 == slot_v[...])
    is_x = row % 8 < 4
    take_x = as_bf16(hit & is_x)
    take_dy = as_bf16(hit & ~is_x)
    row_gate = jnp.sum(jnp.where(hit, gate_v[...], 0.0), axis=1, keepdims=True)
    for copy in copies[3:-2]:
        copy.wait()
    for q in range(quarters):
        got_x = dot(take_x, tok_v[q], ((1,), (0,)))
        got_dy = row_gate * dot(take_dy, cot_v[q], ((1,), (0,)))
        out[q * count : (q + 1) * count] = (got_x + got_dy).astype(bf16)
    for copy in copies[-2:]:
        copy.wait()


def regroup_kernel(place, got, *refs):
    out = refs[-1]
    rows, xs = out.shape[1] // 4, 4
    count = 2 * rows
    n = lax.broadcasted_iota(jnp.int32, (count, count), 0)
    col = lax.broadcasted_iota(jnp.int32, (count, count), 1)
    which, at_l, x, slot = n // rows, (n % rows) // (4 * xs), (n // 4) % xs, n % 4
    perm = as_bf16(col == ((x * (rows // (4 * xs)) + at_l) * 2 + which) * 4 + slot)
    for y in range(4):
        moved = dot(perm, got[y * count : (y + 1) * count], ((1,), (0,))).astype(bf16)
        out[0, y * rows : (y + 1) * rows] = moved[:rows]
        out[1, y * rows : (y + 1) * rows] = moved[rows:]


def halves(place, ref, axis):
    n = ref.shape[axis] // 2
    for c in (core(place), 1 - core(place)):
        part = pl.ds(pl.multiple_of(c * n, n), n)
        yield ref[part, :] if axis == 0 else ref[:, part]


def parts_kernel(place, own, other, w_in, w_out, out):
    hid = w_in.shape[1]
    in_own, in_other = halves(place, w_in, 0)
    out[:, :hid] = (
        dot(own[0], in_own, ((1,), (0,))) + dot(other[0], in_other, ((1,), (0,)))
    ).astype(bf16)
    out_own, out_other = halves(place, w_out, 1)
    out[:, hid:] = (
        dot(own[1], out_own, ((1,), (1,))) + dot(other[1], out_other, ((1,), (1,)))
    ).astype(bf16)


def back_kernel(
    place, got, own, left_a, left_b, right_a, right_b, far_a, far_b, mine, theirs, dh, act, w
):
    hid = dh.shape[1]
    total = got[0].astype(f32)
    for q in range(1, got.shape[0]):
        total = total + got[q].astype(f32)
    gelu_value, gelu_slope = gelu_pair(total[:, :hid])
    dh[...] = (total[:, hid:] * gelu_slope).astype(bf16)
    act[...] = gelu_value.astype(bf16)
    y, c = place[0] >> 1, core(place)
    hs = 4
    f = own.shape[0] // (2 * hs)
    for out, at in ((theirs, 1 - c), (mine, c)):
        for src, q in (
            ((own, own), y),
            ((left_a, left_b), (y + 3) & 3),
            ((right_a, right_b), (y + 1) & 3),
            ((far_a, far_b), (y + 2) & 3),
        ):
            for h in range(hs):
                ref = src[h // 2]
                start = ((h if ref is own else h % 2) * 2 + at) * f
                rows = ref[pl.ds(pl.multiple_of(start, f), f), :]
                w[pl.ds(pl.multiple_of((h * 4 + q) * f, f), f), :] = rows
        out[...] = dot(dh[...], w[...], ((1,), (1,))).astype(out.dtype)


def pack_kernel(place, mine, got, out):
    ls, hs, rows, n = out.shape
    for h in range(hs):
        cols = slice(h * n, (h + 1) * n)
        both = (mine[:, cols] + got[:, cols].astype(f32)).astype(bf16)
        out[:, h] = both.reshape(ls, rows, n)


def sum_kernel(place, got, _, out):
    ls, hs, inner, n = got.shape
    total = got[:, 0].astype(f32)
    for h in range(1, hs):
        total = total + got[:, h].astype(f32)
    rows = ls * inner
    row = lax.broadcasted_iota(jnp.int32, (rows, rows), 0)
    col = lax.broadcasted_iota(jnp.int32, (rows, rows), 1)
    perm = as_bf16(col == (row // 4) % ls * inner + row // (4 * ls) * 4 + row % 4)
    out[...] = dot(perm, total.astype(bf16).reshape(rows, n), ((1,), (0,))).astype(bf16)


def token_kernel(place, eid, slot, got, out):
    quarters, f, toks = out.shape
    row = lax.broadcasted_iota(jnp.int32, (got.shape[0], toks), 0)
    take = as_bf16((row // 4 == eid[...]) & (row % 4 == slot[...]))
    picked = dot(got[...], take, ((0,), (0,))).astype(bf16)
    for q in range(quarters):
        out[q] = picked[q * f : (q + 1) * f]


def grads_kernel(place, own, other, dh, act, g_in, g_out, done):
    done[...] = jnp.zeros_like(done)
    n = own.shape[2]
    for src, c in ((own, core(place)), (other, 1 - core(place))):
        part = pl.ds(pl.multiple_of(c * n, n), n)
        g_in[part, :] = dot(src[0], dh[...], ((0,), (0,))).astype(bf16)
        g_out[:, part] = dot(act[...], src[1], ((0,), (0,))).astype(bf16)


def exchange(x, axes):
    return lax.all_to_all(x, axes, split_axis=0, concat_axis=0, tiled=True)


def other_core(x):
    return lax.ppermute(x, "c", [(0, 1), (1, 0)])


def over_y(x, step):
    return lax.ppermute(x, "y", [(y, (y + step) % 4) for y in range(4)])


def local(tokens, cotangent, gate_value, expert_id, token_slot, w_in, w_out):
    ys, xs, ls, hs = (lax.axis_size(a) for a in ("y", "x", "l", "h"))
    width, hid = w_in.shape[1:]
    toks = tokens.shape[0]
    w_in, w_out = w_in[0], w_out[0]
    eid, slot, gate = (a.reshape(1, toks) for a in (expert_id, token_slot, gate_value))
    groups = ys * xs * ls
    rows, part, f = groups * 4, width // 2, width // 8
    chunk = rows // ys
    sent, w_low, w_high = call(
        dispatch_kernel,
        [((groups * 8, part), bf16)] + [((part, hid), bf16)] * 2,
        eid,
        slot,
        gate,
        tokens,
        cotangent,
        w_in,
        scratch=[
            pltpu.VMEM((1, toks), jnp.int32),
            pltpu.VMEM((1, toks), jnp.int32),
            pltpu.VMEM((1, toks), f32),
            pltpu.VMEM((ys, toks, part), bf16),
            pltpu.VMEM((ys, toks, part), bf16),
            pltpu.SemaphoreType.DMA((5 + 2 * ys,)),
        ],
        fetch=True,
    )
    got = exchange(sent.reshape(groups, 8, part), ("y", "x", "l")).reshape(groups * 8, part)
    right_low, left_high = over_y(w_low, -1), over_y(w_high, 1)
    right_high, left_low = over_y(w_high, -1), over_y(w_low, 1)
    far_low, far_high = over_y(right_low, -1), over_y(left_high, 1)
    gathered = (left_low, left_high, right_low, right_high, far_low, far_high)
    arrived = tuple(a[:16, :128] for a in (left_low, right_high, far_low, far_high)) + (w_out,)
    (own,) = call(regroup_kernel, [((2, rows, part), bf16)], got, after=arrived)
    other = other_core(own)
    (parts,) = call(parts_kernel, [((rows, 2 * hid), bf16)], own, other, w_in, w_out)
    got = exchange(parts.reshape(ys, chunk, 2 * hid), "y")
    block = ((chunk, hid), bf16)
    mine, theirs, dh, act = call(
        back_kernel,
        [((chunk, ys * part), f32), ((chunk, ys * part), bf16), block, block],
        got,
        w_in,
        *gathered,
        scratch=[pltpu.VMEM((ys * part, hid), bf16)],
    )
    got = other_core(theirs)
    (sent,) = call(pack_kernel, [((ls, hs, xs * 4, part), bf16)], mine, got)
    got = exchange(sent.reshape(ls * hs, xs * 4, part), ("l", "h"))
    dh, act = (lax.all_gather(a, "y", axis=0, tiled=True) for a in (dh, act))
    g_in, g_out, done = call(
        grads_kernel,
        [((width, hid), bf16), ((hid, width), bf16), ((8, 128), f32)],
        own,
        other,
        dh,
        act,
    )
    (sent,) = call(
        sum_kernel, [((chunk, part), bf16)], got.reshape(ls, hs, xs * 4, part), after=(done,)
    )
    got = exchange(sent.reshape(xs, ls * 4, part), "x").reshape(chunk, part)
    (grad_t,) = call(token_kernel, [((ys, f, toks), bf16)], eid, slot, got)
    return jnp.transpose(grad_t, (2, 0, 1)), g_in[None], g_out[None]


def solution(mesh):
    dp, expert, mp = mesh.devices.shape
    fine = Mesh(mesh.devices.reshape(dp, 4, expert // 4, mp // 2, 2), ("y", "x", "l", "h", "c"))
    group, ffn = ("y", "x", "l"), ("h", "c")
    in_specs = (
        P(group, None),
        P(group, None),
        P(group),
        P(group),
        P(group),
        P(("x", "l"), "y", ffn),
        P(("x", "l"), ffn, "y"),
    )
    out_specs = (P(group, None, ffn), P(("x", "l"), "y", ffn), P(("x", "l"), ffn, "y"))
    return jax.shard_map(local, mesh=fine, in_specs=in_specs, out_specs=out_specs, check_vma=False)
```

```python
import jax
import jax.numpy as jnp
from jax import lax
from jax.experimental import pallas as pl
from jax.experimental.pallas import tpu as pltpu
from jax.sharding import Mesh, PartitionSpec as P

tanh_scale = 0.7978845608028654
cubic_coef = 0.044715
f32 = jnp.float32
bf16 = jnp.bfloat16


def gelu_pair(pre_act):
    tanh_arg = tanh_scale * (pre_act + cubic_coef * pre_act * pre_act * pre_act)
    tanh_val = jnp.tanh(tanh_arg)
    gelu_value = 0.5 * pre_act * (1.0 + tanh_val)
    gelu_slope = 0.5 * (1.0 + tanh_val) + 0.5 * pre_act * (
        1.0 - tanh_val * tanh_val
    ) * tanh_scale * (1.0 + 3.0 * cubic_coef * pre_act * pre_act)
    return (gelu_value, gelu_slope)


def dot(a, b, dims):
    return lax.dot_general(a, b, ((dims[0], dims[1]), ((), ())), preferred_element_type=f32)


def size(shape):
    n = 1
    for s in shape:
        n *= s
    return n


def call(kernel, outs, *args, scratch=(), fetch=False, lazy=(), after=()):
    moved = sum(a.size * a.dtype.itemsize for a in args) + sum(
        jnp.dtype(d).itemsize * size(s) for s, d in outs
    )
    place = (lax.axis_index("y") * 2 + lax.axis_index("c")).astype(jnp.int32).reshape(1)
    space = pltpu.HBM if fetch else pltpu.VMEM
    return pl.pallas_call(
        kernel,
        out_shape=[jax.ShapeDtypeStruct(s, d) for s, d in outs],
        in_specs=[pl.BlockSpec(memory_space=pltpu.SMEM)]
        + [pl.BlockSpec(memory_space=space)] * len(args)
        + [pl.BlockSpec(memory_space=pltpu.HBM)] * len(lazy)
        + [pl.BlockSpec(memory_space=pl.ANY)] * len(after),
        out_specs=[pl.BlockSpec(memory_space=space)] * len(outs),
        scratch_shapes=scratch,
        compiler_params=pltpu.CompilerParams(vmem_limit_bytes=(60 if fetch else 16) * 1024 * 1024),
        cost_estimate=pl.CostEstimate(flops=0, bytes_accessed=moved, transcendentals=0),
    )(place, *args, *lazy, *after)


def core(place):
    return place[0] & 1


def as_bf16(mask):
    return mask.astype(f32).astype(bf16)


def dispatch_kernel(
    place, eid, slot, gate, tok, cot, w_in, out, w_low, w_high,
    eid_v, slot_v, gate_v, tok_v, cot_v, w_v, out_v, sems, out_sems,
):
    quarters, toks, feats = tok_v.shape
    count = out.shape[0] // quarters
    copies = [
        pltpu.make_async_copy(src, dst, sems.at[i])
        for i, (src, dst) in enumerate(((eid, eid_v), (slot, slot_v), (gate, gate_v)))
    ]
    for q in range(quarters):
        cols = pl.ds(pl.multiple_of((2 * q + core(place)) * feats, feats), feats)
        for src, dst in ((tok, tok_v), (cot, cot_v)):
            copies.append(pltpu.make_async_copy(src.at[:, cols], dst.at[q], sems.at[len(copies)]))
    copies.append(pltpu.make_async_copy(w_in, w_v, sems.at[len(copies)]))
    for copy in copies:
        copy.start()
    for copy in copies[:3]:
        copy.wait()
    row = lax.broadcasted_iota(jnp.int32, (count, toks), 0)
    hit = (row // 8 == eid_v[...]) & (row % 4 == slot_v[...])
    is_x = row % 8 < 4
    take_x = as_bf16(hit & is_x)
    take_dy = as_bf16(hit & ~is_x)
    row_gate = jnp.sum(jnp.where(hit, gate_v[...], 0.0), axis=1, keepdims=True)
    results = []
    for q in range(quarters):
        for copy in copies[3 + 2 * q : 5 + 2 * q]:
            copy.wait()
        got_x = dot(take_x, tok_v[q], ((1,), (0,)))
        got_dy = row_gate * dot(take_dy, cot_v[q], ((1,), (0,)))
        out_v[q] = (got_x + got_dy).astype(bf16)
        dst = out.at[q * count : (q + 1) * count]
        results.append(pltpu.make_async_copy(out_v.at[q], dst, out_sems.at[q]))
        results[-1].start()
    copies[-1].wait()
    half = w_in.shape[0] // 2
    for i, dst in enumerate((w_low, w_high)):
        src = w_v.at[i * half : (i + 1) * half]
        results.append(pltpu.make_async_copy(src, dst, out_sems.at[quarters + i]))
        results[-1].start()
    for copy in results:
        copy.wait()


def regroup_kernel(place, got, *refs):
    out = refs[-1]
    rows, xs = out.shape[1] // 4, 4
    count = 2 * rows
    n = lax.broadcasted_iota(jnp.int32, (count, count), 0)
    col = lax.broadcasted_iota(jnp.int32, (count, count), 1)
    which, at_l, x, slot = n // rows, (n % rows) // (4 * xs), (n // 4) % xs, n % 4
    perm = as_bf16(col == ((x * (rows // (4 * xs)) + at_l) * 2 + which) * 4 + slot)
    for y in range(4):
        moved = dot(perm, got[y * count : (y + 1) * count], ((1,), (0,))).astype(bf16)
        out[0, y * rows : (y + 1) * rows] = moved[:rows]
        out[1, y * rows : (y + 1) * rows] = moved[rows:]


def halves(place, ref, axis):
    n = ref.shape[axis] // 2
    for c in (core(place), 1 - core(place)):
        part = pl.ds(pl.multiple_of(c * n, n), n)
        yield ref[part, :] if axis == 0 else ref[:, part]


def parts_kernel(place, own, other, w_in, w_out, out):
    hid = w_in.shape[1]
    in_own, in_other = halves(place, w_in, 0)
    out[:, :hid] = (
        dot(own[0], in_own, ((1,), (0,))) + dot(other[0], in_other, ((1,), (0,)))
    ).astype(bf16)
    out_own, out_other = halves(place, w_out, 1)
    out[:, hid:] = (
        dot(own[1], out_own, ((1,), (1,))) + dot(other[1], out_other, ((1,), (1,)))
    ).astype(bf16)


def back_kernel(
    place, got, own, left_a, left_b, right_a, right_b, far_a, far_b, mine, theirs, dh, act, w, sems
):
    y, c = place[0] >> 1, core(place)
    hs = 4
    f = own.shape[0] // (2 * hs)
    copies = []
    for i, at in enumerate((1 - c, c)):
        for src, q in (
            ((own, own), y),
            ((left_a, left_b), (y + 3) & 3),
            ((right_a, right_b), (y + 1) & 3),
            ((far_a, far_b), (y + 2) & 3),
        ):
            for h in range(hs):
                ref = src[h // 2]
                start = ((h if ref is own else h % 2) * 2 + at) * f
                rows = ref.at[pl.ds(pl.multiple_of(start, f), f)]
                place_in_w = w.at[i, pl.ds(pl.multiple_of((h * 4 + q) * f, f), f)]
                copies.append(pltpu.make_async_copy(rows, place_in_w, sems.at[len(copies)]))
    for copy in copies:
        copy.start()
    hid = dh.shape[1]
    total = got[0].astype(f32)
    for q in range(1, got.shape[0]):
        total = total + got[q].astype(f32)
    gelu_value, gelu_slope = gelu_pair(total[:, :hid])
    dh[...] = (total[:, hid:] * gelu_slope).astype(bf16)
    act[...] = gelu_value.astype(bf16)
    for i, out in enumerate((theirs, mine)):
        for copy in copies[16 * i : 16 * (i + 1)]:
            copy.wait()
        out[...] = dot(dh[...], w[i], ((1,), (1,))).astype(out.dtype)


def pack_kernel(place, mine, got, out):
    ls, hs, rows, n = out.shape
    for h in range(hs):
        cols = slice(h * n, (h + 1) * n)
        both = (mine[:, cols] + got[:, cols].astype(f32)).astype(bf16)
        out[:, h] = both.reshape(ls, rows, n)


def sum_kernel(place, got, _, out):
    ls, hs, inner, n = got.shape
    total = got[:, 0].astype(f32)
    for h in range(1, hs):
        total = total + got[:, h].astype(f32)
    rows = ls * inner
    row = lax.broadcasted_iota(jnp.int32, (rows, rows), 0)
    col = lax.broadcasted_iota(jnp.int32, (rows, rows), 1)
    perm = as_bf16(col == (row // 4) % ls * inner + row // (4 * ls) * 4 + row % 4)
    out[...] = dot(perm, total.astype(bf16).reshape(rows, n), ((1,), (0,))).astype(bf16)


def token_kernel(place, eid, slot, got, out):
    quarters, f, toks = out.shape
    row = lax.broadcasted_iota(jnp.int32, (got.shape[0], toks), 0)
    take = as_bf16((row // 4 == eid[...]) & (row % 4 == slot[...]))
    picked = dot(got[...], take, ((0,), (0,))).astype(bf16)
    for q in range(quarters):
        out[q] = picked[q * f : (q + 1) * f]


def grads_kernel(place, own, other, dh, act, g_in, g_out, done):
    done[...] = jnp.zeros_like(done)
    n = own.shape[2]
    for src, c in ((own, core(place)), (other, 1 - core(place))):
        part = pl.ds(pl.multiple_of(c * n, n), n)
        g_in[part, :] = dot(src[0], dh[...], ((0,), (0,))).astype(bf16)
        g_out[:, part] = dot(act[...], src[1], ((0,), (0,))).astype(bf16)


def exchange(x, axes):
    return lax.all_to_all(x, axes, split_axis=0, concat_axis=0, tiled=True)


def other_core(x):
    return lax.ppermute(x, "c", [(0, 1), (1, 0)])


def over_y(x, step):
    return lax.ppermute(x, "y", [(y, (y + step) % 4) for y in range(4)])


def local(tokens, cotangent, gate_value, expert_id, token_slot, w_in, w_out):
    ys, xs, ls, hs = (lax.axis_size(a) for a in ("y", "x", "l", "h"))
    width, hid = w_in.shape[1:]
    toks = tokens.shape[0]
    w_in, w_out = w_in[0], w_out[0]
    eid, slot, gate = (a.reshape(1, toks) for a in (expert_id, token_slot, gate_value))
    groups = ys * xs * ls
    rows, part, f = groups * 4, width // 2, width // 8
    chunk = rows // ys
    sent, w_low, w_high = call(
        dispatch_kernel,
        [((groups * 8, part), bf16)] + [((part, hid), bf16)] * 2,
        eid,
        slot,
        gate,
        tokens,
        cotangent,
        w_in,
        scratch=[
            pltpu.VMEM((1, toks), jnp.int32),
            pltpu.VMEM((1, toks), jnp.int32),
            pltpu.VMEM((1, toks), f32),
            pltpu.VMEM((ys, toks, part), bf16),
            pltpu.VMEM((ys, toks, part), bf16),
            pltpu.VMEM(w_in.shape, bf16),
            pltpu.VMEM((ys, groups * 8 // ys, part), bf16),
            pltpu.SemaphoreType.DMA((4 + 2 * ys,)),
            pltpu.SemaphoreType.DMA((ys + 2,)),
        ],
        fetch=True,
    )
    got = exchange(sent.reshape(groups, 8, part), ("y", "x", "l")).reshape(groups * 8, part)
    right_low, left_high = over_y(w_low, -1), over_y(w_high, 1)
    right_high, left_low = over_y(w_high, -1), over_y(w_low, 1)
    far_low, far_high = over_y(right_low, -1), over_y(left_high, 1)
    gathered = (left_low, left_high, right_low, right_high, far_low, far_high)
    arrived = tuple(a[:16, :128] for a in (left_low, right_high, far_low, far_high)) + (w_out,)
    (own,) = call(regroup_kernel, [((2, rows, part), bf16)], got, after=arrived)
    other = other_core(own)
    (parts,) = call(parts_kernel, [((rows, 2 * hid), bf16)], own, other, w_in, w_out)
    got = exchange(parts.reshape(ys, chunk, 2 * hid), "y")
    block = ((chunk, hid), bf16)
    mine, theirs, dh, act = call(
        back_kernel,
        [((chunk, ys * part), f32), ((chunk, ys * part), bf16), block, block],
        got,
        scratch=[pltpu.VMEM((2, ys * part, hid), bf16), pltpu.SemaphoreType.DMA((32,))],
        lazy=(w_in,) + gathered,
    )
    got = other_core(theirs)
    (sent,) = call(pack_kernel, [((ls, hs, xs * 4, part), bf16)], mine, got)
    got = exchange(sent.reshape(ls * hs, xs * 4, part), ("l", "h"))
    dh, act = (lax.all_gather(a, "y", axis=0, tiled=True) for a in (dh, act))
    g_in, g_out, done = call(
        grads_kernel,
        [((width, hid), bf16), ((hid, width), bf16), ((8, 128), f32)],
        own,
        other,
        dh,
        act,
    )
    (sent,) = call(
        sum_kernel, [((chunk, part), bf16)], got.reshape(ls, hs, xs * 4, part), after=(done,)
    )
    got = exchange(sent.reshape(xs, ls * 4, part), "x").reshape(chunk, part)
    (grad_t,) = call(token_kernel, [((ys, f, toks), bf16)], eid, slot, got)
    return jnp.transpose(grad_t, (2, 0, 1)), g_in[None], g_out[None]


def solution(mesh):
    dp, expert, mp = mesh.devices.shape
    fine = Mesh(mesh.devices.reshape(dp, 4, expert // 4, mp // 2, 2), ("y", "x", "l", "h", "c"))
    group, ffn = ("y", "x", "l"), ("h", "c")
    in_specs = (
        P(group, None),
        P(group, None),
        P(group),
        P(group),
        P(group),
        P(("x", "l"), "y", ffn),
        P(("x", "l"), ffn, "y"),
    )
    out_specs = (P(group, None, ffn), P(("x", "l"), "y", ffn), P(("x", "l"), ffn, "y"))
    return jax.shard_map(local, mesh=fine, in_specs=in_specs, out_specs=out_specs, check_vma=False)
```
